256 devices in a mesh: ctx: 16 (over y_lo, x, core), fsdp: 16 (over z, y_hi).
Axes of the slice: x: 4, y: 4 (y_hi: 2, y_lo: 2; y = y_hi * 2 + y_lo), z: 8, core: 2. Of those that a mesh axis runs over, the one named last changes fastest.
Arguments:
- x_t: bfloat16 [32, 1024, 1536], P('fsdp', 'ctx'), may hold values from -6 to 6
- clip_len: int32 [32], P('fsdp'), may hold values from 1 to 1024, as said below
- time_idx: int32 [32], P('fsdp'), may hold values from 0 to 999
- teacher_mod: float32 [2, 1536], replicated, may hold values from -2 to 2
- student_mod: float32 [2, 1536], replicated, may hold values from -2 to 2
- w_qkv: bfloat16 [1536, 6144], P('fsdp'), may hold values from -1 to 1
- w_out: bfloat16 [2048, 1536], P('fsdp'), may hold values from -0.125 to 0.125
Outputs:
- student_out: bfloat16 [32, 1024, 1536], P('fsdp', 'ctx')
- student_tangent: bfloat16 [32, 1024, 1536], P('fsdp', 'ctx')
The draws below stay inside these ranges and needn't reach their ends.
Inputs may be any that keep to these rules, and one draw needn't show every extreme that they name: `clip_len`: every draw has a clip of exactly 1024 live tokens and a short clip of at most 128.
All inputs are finite; a program needn't handle non-finite values.
Results may differ from the reference program's by a relative error of at most 0.015.
The reference program's roundings to bfloat16 on the way count: a program that leaves them out, or rounds other values in their place, can miss the bound.
Values may be sent and summed in bfloat16 or wider, within the bound.
A program may use at most 128 MiB of HBM per device.

```python
import math
import jax
import jax.numpy as jnp
from jax import lax

D = 1536
HEADS = 16
HD = 128
TIME_STEPS = 1000
INNER = 2048
SLOT = 1024
CLIPS = 32


def draw_clip_len(key, part):
    key = jax.random.fold_in(key, 11)
    first, second, third, fourth = jax.random.split(key, 4)
    lengths = jax.random.randint(first, (CLIPS,), SLOT // 2, SLOT + 1)
    full_pick = jax.random.randint(second, (), 0, CLIPS)
    short_pick = (full_pick + 1 + jax.random.randint(third, (), 0, CLIPS - 1)) % CLIPS
    lengths = lengths.at[short_pick].set(jax.random.randint(fourth, (), 1, SLOT // 8 + 1))
    lengths = lengths.at[full_pick].set(SLOT)
    return lengths.astype(jnp.int32)


def draw_w_qkv(key, part):
    key = jax.random.fold_in(key, 23)
    base_key = jax.random.fold_in(key, 0)
    base = jnp.clip(jax.random.normal(base_key, (D, 3 * INNER), jnp.float32), -4.0, 4.0)
    weight = base * D ** (-0.5)
    return weight.astype(jnp.bfloat16)


def plant(result, own_key, smallest, top_value):
    place = [jax.random.randint(jax.random.fold_in(own_key, axis), (), 0, length) for axis, length in enumerate(result.shape)]
    longest = result.shape.index(max(result.shape))
    next_to = place[:longest] + [(place[longest] + 1) % result.shape[longest]] + place[longest + 1:]
    return result.at[tuple(place)].set(smallest).at[tuple(next_to)].set(top_value)


def block_scale(own_key, dims, shards, low, largest):
    factor_of = 1.0
    for dim, blocks in shards:
        draws = jax.random.uniform(jax.random.fold_in(jax.random.fold_in(own_key, 6), dim), (blocks,), jnp.float32, low / len(shards), largest / len(shards))
        factor_of = factor_of * jnp.repeat(jnp.exp(draws), dims[dim] // blocks).reshape((-1,) + (1,) * (len(dims) - 1 - dim))
    return factor_of


def normal_values(key, extent, scale, most, cuts=(), kind=jnp.bfloat16):
    factor_of = block_scale(key, extent, cuts, -0.22, 0.18) if cuts else 1.0
    values = jax.random.normal(key, extent, jnp.float32) * scale * factor_of
    return jnp.minimum(jnp.maximum(values, -most), most).astype(kind)


def setup_inputs(seed: int = 0) -> dict:
    seeds = jax.random.split(jax.random.key(seed), 8)
    x_t = normal_values(seeds[0], (CLIPS, SLOT, D), 1.0, 6.0, ((0, 16), (1, 16)))
    clip_len = draw_clip_len(jax.random.fold_in(seeds[7], 71), 0)
    time_idx = plant(jax.random.randint(seeds[2], (CLIPS,), 0, TIME_STEPS), jax.random.fold_in(seeds[2], 1), 0, TIME_STEPS - 1).astype(jnp.int32)
    teacher_mod = normal_values(seeds[3], (2, D), 0.4, 2.0, (), jnp.float32)
    student_mod = normal_values(seeds[4], (2, D), 0.4, 2.0, (), jnp.float32)
    w_qkv = draw_w_qkv(jax.random.fold_in(seeds[7], 71), 0)
    w_out = normal_values(seeds[6], (INNER, D), INNER ** -0.5, 0.125, ((0, 16),))
    return dict(x_t=x_t, clip_len=clip_len, time_idx=time_idx, teacher_mod=teacher_mod, student_mod=student_mod, w_qkv=w_qkv, w_out=w_out)


def softmax_parts(query, keys, live):
    scale = 1.0 / math.sqrt(HD)
    scores = jnp.einsum('qhd,khd->hqk', query.astype(jnp.float32), keys.astype(jnp.float32)) * scale
    scores = jnp.where(live[None, None, :], scores, -1e+30)
    top = lax.optimization_barrier(jnp.max(scores, axis=-1, keepdims=True))
    expo = jnp.exp(scores - top)
    probs = expo / lax.optimization_barrier(jnp.sum(expo, axis=-1, keepdims=True))
    return (probs, probs.astype(jnp.bfloat16))

def attend(packed, live):
    query, keys, values = (packed[:, 0], packed[:, 1], packed[:, 2])
    probs, weights = softmax_parts(query, keys, live)
    out = jnp.einsum('hqk,khd->qhd', weights.astype(jnp.float32), values.astype(jnp.float32))
    return out.astype(jnp.bfloat16)

def attend_tangent(packed, tangent, live):
    scale = 1.0 / math.sqrt(HD)
    query, keys, values = (packed[:, 0], packed[:, 1], packed[:, 2])
    dquery, dkeys, dvalues = (tangent[:, 0], tangent[:, 1], tangent[:, 2])
    probs, weights = softmax_parts(query, keys, live)
    out = jnp.einsum('hqk,khd->qhd', weights.astype(jnp.float32), values.astype(jnp.float32))
    dscore = jnp.einsum('qhd,khd->hqk', dquery.astype(jnp.float32), keys.astype(jnp.float32))
    dscore = (dscore + jnp.einsum('qhd,khd->hqk', query.astype(jnp.float32), dkeys.astype(jnp.float32))) * scale
    dprob = probs * (dscore - lax.optimization_barrier(jnp.sum(probs * dscore, axis=-1, keepdims=True)))
    dout = jnp.einsum('hqk,khd->qhd', dprob.astype(jnp.bfloat16).astype(jnp.float32), values.astype(jnp.float32))
    dout = dout + jnp.einsum('hqk,khd->qhd', weights.astype(jnp.float32), dvalues.astype(jnp.float32))
    return (out.astype(jnp.bfloat16), dout.astype(jnp.bfloat16))

def reference(x_t, clip_len, time_idx, teacher_mod, student_mod, w_qkv, w_out):

    def one_clip(args):
        latent, length, index = args
        angle = math.pi / 2 * (index.astype(jnp.float32) + 0.5) / TIME_STEPS
        sin_t = jnp.sin(angle)
        cos_t = jnp.cos(angle)
        live = jnp.arange(SLOT, dtype=jnp.int32) < length
        latent_f = latent.astype(jnp.float32)
        rstd = lax.rsqrt(lax.optimization_barrier(jnp.mean(latent_f * latent_f, axis=-1, keepdims=True)) + 1e-06)
        normed = latent_f * rstd
        gain_teacher = 1.0 + sin_t * teacher_mod[0] + cos_t * teacher_mod[1]
        h_teacher = (normed * gain_teacher).astype(jnp.bfloat16)
        qkv_teacher = jnp.dot(h_teacher, w_qkv, preferred_element_type=jnp.float32).astype(jnp.bfloat16)
        attn_teacher = attend(qkv_teacher.reshape(SLOT, 3, HEADS, HD), live)
        velocity = jnp.dot(attn_teacher.reshape(SLOT, INNER), w_out, preferred_element_type=jnp.float32).astype(jnp.bfloat16)
        gain_student = 1.0 + sin_t * student_mod[0] + cos_t * student_mod[1]
        dgain_student = cos_t * student_mod[0] - sin_t * student_mod[1]
        h_student = (normed * gain_student).astype(jnp.bfloat16)
        vel_f = velocity.astype(jnp.float32)
        cross = lax.optimization_barrier(jnp.mean(latent_f * vel_f, axis=-1, keepdims=True))
        dnormed = rstd * vel_f - latent_f * rstd * rstd * rstd * cross
        dh_student = (dnormed * gain_student + normed * dgain_student).astype(jnp.bfloat16)
        qkv_student = jnp.dot(h_student, w_qkv, preferred_element_type=jnp.float32).astype(jnp.bfloat16)
        dqkv_student = jnp.dot(dh_student, w_qkv, preferred_element_type=jnp.float32).astype(jnp.bfloat16)
        attn_student, dattn_student = attend_tangent(qkv_student.reshape(SLOT, 3, HEADS, HD), dqkv_student.reshape(SLOT, 3, HEADS, HD), live)
        student_out = jnp.dot(attn_student.reshape(SLOT, INNER), w_out, preferred_element_type=jnp.float32).astype(jnp.bfloat16)
        student_tangent = jnp.dot(dattn_student.reshape(SLOT, INNER), w_out, preferred_element_type=jnp.float32).astype(jnp.bfloat16)
        return (student_out, student_tangent)
    student_out, student_tangent = lax.map(one_clip, (x_t, clip_len, time_idx))
    return (student_out, student_tangent)
```

```python
import functools
import math

import jax
import jax.numpy as jnp
from jax import lax
from jax.experimental import pallas as pl
from jax.experimental.pallas import tpu as pltpu
from jax.sharding import PartitionSpec as P

HEADS = 16
HD = 128
TIME_STEPS = 1000
D = 1536
INNER = HEADS * HD
SEG = 64
CLIPS = 2
SLOTS = 8
HALF = SLOTS * SEG
FULL = 2 * HALF
BLK = 4 * SEG
SCALE = 1.0 / math.sqrt(HD)
EXP2_SCALE = SCALE * math.log2(math.e)
MESH = pl.DeviceIdType.MESH
F32 = jnp.float32
BF16 = jnp.bfloat16

S00, S01, S03, S10, S02, S11, S13, S12 = range(8)


def mult(value, by):
    return pl.multiple_of(value, by)


def kernel(
    len_ref, time_ref, x_ref, tmod_ref, smod_ref, wqkv_ref, wout_ref,
    student_ref, tangent_ref,
    xg, dg, wq, wo, qkv_t, qkv_s, qkv_d, other_t, other_s, other_d, hbuf, gains, kmask,
    mixed_t, mixed_s, mixed_d, attn_t, attn_s, attn_d, vel, dh, scaled, weights,
    send, recv, local, bulk_send, bulk_recv,
):
    c = lax.axis_index("ctx")
    f = lax.axis_index("fsdp")
    core = c % 2
    chip = c // 2
    xx = chip % 4
    yl = c // 8
    z = f // 2
    yh = f % 2

    def device(dcore=0, dx=0, dyl=0, dz=0, dyh=0):
        ctx = ((yl + dyl) % 2 * 4 + (xx + dx) % 4) * 2 + (core + dcore) % 2
        return (ctx, (z + dz) % 8 * 2 + (yh + dyh) % 2)

    sibling = device(dcore=1)
    x_up, x_down = device(dx=1), device(dx=3)
    y_in = device(dyl=1)
    y_out = device(dyl=1, dyh=1)
    z_up, z_down = device(dz=1), device(dz=7)

    barrier = pltpu.get_barrier_semaphore()
    partners = [y_out, z_up, z_down]
    for dyl in range(2):
        for dx in range(4):
            for dcore in range(2):
                if dyl + dx + dcore:
                    partners.append(device(dcore=dcore, dx=dx, dyl=dyl))
    for partner in partners:
        pl.semaphore_signal(barrier, inc=1, device_id=partner, device_id_type=MESH)

    used = [0]
    started = []

    def remote(src, dst, where):
        number = used[0]
        used[0] += 1
        copy = pltpu.make_async_remote_copy(
            src_ref=src, dst_ref=dst, send_sem=send.at[number], recv_sem=recv.at[number],
            device_id=where, device_id_type=MESH,
        )
        copy.start()
        started.append(copy)
        return copy

    nlocal = [0]

    def here(src, dst):
        copy = pltpu.make_async_copy(src, dst, local.at[nlocal[0]])
        nlocal[0] += 1
        copy.start()
        return copy

    def arrived(*copies):
        for copy in copies:
            copy.wait_recv()

    class Gather:
        def __init__(self, own, buf):
            self.own, self.buf = own, buf

        def slot(self, clip, slot, lo=0, n=SEG):
            return self.buf.at[pl.ds(clip * HALF + slot * SEG + lo, n)]

        def mine(self, clip):
            return self.own.at[pl.ds(clip * SEG, SEG)]

        def begin(self):
            self.b_up = remote(self.mine(1), self.slot(1, S03), x_up)
            self.b_down = remote(self.mine(1), self.slot(1, S01), x_down)
            self.a_y = remote(self.mine(0), self.slot(0, S10), y_in)
            self.a_up = remote(self.mine(0), self.slot(0, S03), x_up)
            self.a_down = remote(self.mine(0), self.slot(0, S01), x_down)
            self.b_y = remote(self.mine(1), self.slot(1, S10), y_in)
            self.self0 = here(self.mine(0), self.slot(0, S00))
            self.self1 = here(self.mine(1), self.slot(1, S00))

        def step1(self):
            arrived(self.b_up)
            self.b_h_up = remote(self.slot(1, S03, 0, 32), self.slot(1, S02, 0, 32), x_up)
            arrived(self.b_down)
            self.b_h_down = remote(self.slot(1, S01, 32, 32), self.slot(1, S02, 32, 32), x_down)
            self.b_y1 = remote(self.slot(1, S01), self.slot(1, S11), y_in)
            self.b_y3 = remote(self.slot(1, S03), self.slot(1, S13), y_in)

        def step2(self):
            arrived(self.a_y)
            self.a_y_up = remote(self.slot(0, S10), self.slot(0, S13), x_up)
            self.a_y_down = remote(self.slot(0, S10), self.slot(0, S11), x_down)

        def step3(self):
            arrived(self.a_up)
            self.a_h_up = remote(self.slot(0, S03, 0, 32), self.slot(0, S02, 0, 32), x_up)
            arrived(self.a_down)
            self.a_h_down = remote(self.slot(0, S01, 32, 32), self.slot(0, S02, 32, 32), x_down)

        def step4(self):
            arrived(self.b_h_up, self.b_h_down)
            self.b_y2 = remote(self.slot(1, S02), self.slot(1, S12), y_in)
            arrived(self.b_y)
            self.self0.wait()
            self.self1.wait()

        def step5(self):
            arrived(self.a_y_up)
            self.a_yh_up = remote(self.slot(0, S13, 0, 32), self.slot(0, S12, 0, 32), x_up)
            arrived(self.a_y_down)
            self.a_yh_down = remote(self.slot(0, S11, 32, 32), self.slot(0, S12, 32, 32), x_down)

        def end_a(self):
            arrived(self.a_h_up, self.a_h_down, self.a_yh_up, self.a_yh_down)

        def end_b(self):
            arrived(self.b_y1, self.b_y3, self.b_y2)

    class Ring:
        def __init__(self, buf, rows, cols, core_cols):
            self.buf, self.rows, self.cols, self.core_cols = buf, rows, cols, core_cols
            self.cores = []

        def block(self, dz, part=None):
            base = mult((z + dz) % 8 * (2 * self.rows), 16)
            if part is None:
                return self.buf.at[pl.ds(base, 2 * self.rows), self.cols]
            return self.buf.at[pl.ds(base + part * self.rows, self.rows), self.cols]

        def share(self, dz):
            base = mult((z + dz) % 8 * (2 * self.rows), 16)
            self.cores.append(remote(
                self.block(dz), self.buf.at[pl.ds(base, 2 * self.rows), self.core_cols], sibling))

        def step1(self):
            self.up = remote(self.block(0), self.block(0), z_up)
            self.down = remote(self.block(0), self.block(0), z_down)
            self.share(0)

        def step(self, k):
            arrived(self.up)
            if k < 4:
                self.up = remote(self.block(-k + 1), self.block(-k + 1), z_up)
            arrived(self.down)
            if k < 4:
                self.down = remote(self.block(k - 1), self.block(k - 1), z_down)
            self.share(8 - k + 1)
            self.share(k - 1)

        def step4(self):
            arrived(self.up)
            self.up = remote(self.block(-3, 0), self.block(-3, 0), z_up)
            arrived(self.down)
            self.down = remote(self.block(3, 1), self.block(3, 1), z_down)
            self.share(5)
            self.share(3)

        def last(self):
            arrived(self.up, self.down)
            self.share(4)

        def end(self):
            arrived(*self.cores)

    pl.semaphore_wait(barrier, len(partners))

    gx = Gather(x_ref, xg)
    gx.begin()
    c_out = (c + 8) % 16
    row_q = mult(f * 96, 16)
    hop_q = [
        remote(
            wqkv_ref.at[:, pl.ds(mult(part * INNER + c_out * HD, HD), HD)],
            wq.at[pl.ds(row_q, 96), pl.ds(part * HD, HD)], y_out)
        for part in range(3)
    ]
    own_q = [
        here(
            wqkv_ref.at[:, pl.ds(mult(part * INNER + c * HD, HD), HD)],
            wq.at[pl.ds(row_q, 96), pl.ds(part * HD, HD)])
        for part in range(3)
    ]
    my_cols = pl.ds(mult(core * 768, HD), 768)
    row_o = mult(f * HD, HD)
    hop_o = remote(wout_ref.at[:, my_cols], wo.at[pl.ds(row_o, HD), my_cols], y_out)
    own_o = here(wout_ref.at[:, my_cols], wo.at[pl.ds(row_o, HD), my_cols])
    rq = Ring(wq, 96, pl.ds(0, 384), pl.ds(384, 384))
    ro = Ring(wo, HD, my_cols, my_cols)

    for clip in range(CLIPS):
        angle = jnp.full((1, D), time_ref[clip].astype(F32), F32)
        angle = math.pi / 2 * (angle + 0.5) / TIME_STEPS
        sin_t, cos_t = jnp.sin(angle), jnp.cos(angle)
        gains[pl.ds(clip * 3, 1)] = 1.0 + sin_t * tmod_ref[0:1] + cos_t * tmod_ref[1:2]
        gains[pl.ds(clip * 3 + 1, 1)] = 1.0 + sin_t * smod_ref[0:1] + cos_t * smod_ref[1:2]
        gains[pl.ds(clip * 3 + 2, 1)] = cos_t * smod_ref[0:1] - sin_t * smod_ref[1:2]
    within = lax.broadcasted_iota(jnp.int32, (SEG, HD), 0)
    lane0 = lax.broadcasted_iota(jnp.int32, (SEG, HD), 1) == 0
    places = ((0, 0), (0, 1), (0, 3), (1, 0), (0, 2), (1, 1), (1, 3), (1, 2))
    for clip in range(CLIPS):
        for half in range(2):
            for slot, (dyl, dx) in enumerate(places):
                token = within + device(dcore=half, dx=dx, dyl=dyl)[0] * SEG
                dead = jnp.logical_and(token >= len_ref[clip], lane0)
                kmask[pl.ds(clip * FULL + half * HALF + slot * SEG, SEG)] = jnp.where(
                    dead, -1e30, 0.0).astype(BF16)
    one0 = jnp.where(lax.broadcasted_iota(jnp.int32, (BLK, HD), 1) == 0, 1.0, 0.0).astype(BF16)

    def project(source, base, out, other):
        y = jnp.dot(source, wq[...], preferred_element_type=F32).astype(BF16)
        clip, rest = base // HALF, base % HALF
        out[pl.ds(mult(clip * FULL + rest, BLK), BLK)] = y[:, :384]
        other[pl.ds(mult(base, BLK), BLK)] = y[:, 384:]

    def chunk(base, gain_row, out, other):
        def piece(i, _):
            xf = xg[pl.ds(mult(base + i * 32, 32), 32)].astype(F32)
            rstd = lax.rsqrt(jnp.mean(xf * xf, axis=-1, keepdims=True) + 1e-6)
            hbuf[pl.ds(mult(i * 32, 32), 32)] = (xf * rstd * gains[pl.ds(gain_row, 1)]).astype(BF16)
            return 0

        lax.fori_loop(0, BLK // 32, piece, 0)
        project(hbuf[...], base, out, other)

    def exchange(clip, group, out, other):
        return remote(
            other.at[pl.ds(clip * HALF + group * BLK, BLK)],
            out.at[pl.ds(clip * FULL + HALF + group * BLK, BLK)], sibling)

    def send_block(blk, phase, mixed, attn):
        clip = blk // 4
        half = blk // 2 % 2
        group = blk % 2
        steps = ((0, 2 * group), (group, 1), (group, 3), (1, 2 * group))
        for j, (dyl, dx) in enumerate(steps):
            where = device(dcore=half, dx=dx, dyl=dyl)
            src = mixed.at[pl.ds(mult(blk * BLK + j * SEG, SEG), SEG)]
            dst = attn.at[pl.ds(mult(clip * SEG, SEG), SEG), pl.ds(mult(c * HD, HD), HD)]

            def away(src=src, dst=dst, where=where):
                pltpu.make_async_remote_copy(
                    src_ref=src, dst_ref=dst, send_sem=bulk_send.at[phase],
                    recv_sem=bulk_recv.at[phase], device_id=where, device_id_type=MESH,
                ).start()

            if j == 0:
                stays = half + group == 0

                @pl.when(stays)
                def _(src=src, dst=dst):
                    pltpu.make_async_copy(src, dst, bulk_recv.at[phase]).start()

                pl.when(jnp.logical_not(stays))(away)
            else:
                away()

    def all_received(phase, attn):
        pltpu.make_async_copy(attn, attn, bulk_recv.at[phase]).wait()

    def all_sent(phase, attn):
        part = attn.at[:, pl.ds(0, INNER - HD)]
        pltpu.make_async_copy(part, part, bulk_send.at[phase]).wait()

    NT = (((1,), (1,)), ((), ()))

    def scores_of(blk, qkv):
        clip = blk // 4
        rows = pl.ds(mult(blk * BLK, BLK), BLK)
        keys = pl.ds(mult(clip * FULL, FULL), FULL)
        query = jnp.concatenate([qkv[rows, 0:HD], one0], axis=1)
        key = jnp.concatenate([qkv[keys, HD:2 * HD], kmask[keys]], axis=1)
        scores = lax.dot_general(query, key, NT, preferred_element_type=F32)
        top = jnp.max(scores, axis=-1, keepdims=True)
        expo = jnp.exp2((scores - top) * EXP2_SCALE)
        return rows, keys, expo, jnp.sum(expo, axis=-1, keepdims=True)

    def teacher_block(blk, _):
        rows, keys, expo, total = scores_of(blk, qkv_t)
        out = jnp.dot(expo.astype(BF16), qkv_t[keys, 2 * HD:], preferred_element_type=F32)
        mixed_t[rows] = (out / total).astype(BF16)
        send_block(blk, 0, mixed_t, attn_t)
        return 0

    def student_block(blk, _):
        rows, keys, expo, total = scores_of(blk, qkv_s)
        probs = expo * (1.0 / total)
        weight = probs.astype(BF16)
        weights[rows] = weight
        scaled[rows] = probs * SCALE
        mixed_s[rows] = jnp.dot(
            weight, qkv_s[keys, 2 * HD:], preferred_element_type=F32).astype(BF16)
        return 0

    def tangent_block(blk, _):
        clip = blk // 4
        rows = pl.ds(mult(blk * BLK, BLK), BLK)
        keys = pl.ds(mult(clip * FULL, FULL), FULL)
        query = jnp.concatenate([qkv_d[rows, 0:HD], qkv_s[rows, 0:HD]], axis=1)
        key = jnp.concatenate([qkv_s[keys, HD:2 * HD], qkv_d[keys, HD:2 * HD]], axis=1)
        dscore = lax.dot_general(query, key, NT, preferred_element_type=F32)
        prob = scaled[rows]
        mean = jnp.sum(prob * dscore, axis=-1, keepdims=True) * (1.0 / SCALE)
        dprob = (prob * (dscore - mean)).astype(BF16)
        out = jnp.dot(dprob, qkv_s[keys, 2 * HD:], preferred_element_type=F32)
        out += jnp.dot(weights[rows], qkv_d[keys, 2 * HD:], preferred_element_type=F32)
        mixed_d[rows] = out.astype(BF16)
        send_block(blk, 2, mixed_d, attn_d)
        return 0

    def output(attn, out):
        def tile(n, _):
            cols = pl.ds(mult(n * 512, 512), 512)
            out[:, cols] = jnp.dot(
                attn[...], wo[:, cols], preferred_element_type=F32).astype(BF16)
            return 0

        lax.fori_loop(0, 3, tile, 0)

    arrived(*hop_q)
    for copy in own_q:
        copy.wait()
    rq.step1()
    gx.step1()
    gx.step2()
    rq.step(2)
    gx.step3()
    rq.step(3)
    gx.step4()
    rq.step4()
    arrived(hop_o)
    own_o.wait()
    gx.step5()
    rq.last()
    ro.step1()
    rq.end()

    def early(clip, _):
        base = clip * HALF
        chunk(base, clip * 3, qkv_t, other_t)
        chunk(base, clip * 3 + 1, qkv_s, other_s)
        return 0

    def late_teacher(clip, _):
        chunk(clip * HALF + BLK, clip * 3, qkv_t, other_t)
        return 0

    def late_student(clip, _):
        chunk(clip * HALF + BLK, clip * 3 + 1, qkv_s, other_s)
        return 0

    lax.fori_loop(0, 2, early, 0)
    swaps_t = [exchange(clip, 0, qkv_t, other_t) for clip in range(2)]
    swaps_s = [exchange(clip, 0, qkv_s, other_s) for clip in range(2)]
    gx.end_a()
    gx.end_b()
    lax.fori_loop(0, 2, late_teacher, 0)
    swaps_t += [exchange(clip, 1, qkv_t, other_t) for clip in range(2)]
    lax.fori_loop(0, 2, late_student, 0)
    swaps_s += [exchange(clip, 1, qkv_s, other_s) for clip in range(2)]
    ro.step(2)
    arrived(*swaps_t)
    lax.fori_loop(0, 8, teacher_block, 0)
    ro.step(3)
    arrived(*swaps_s)
    lax.fori_loop(0, 8, student_block, 0)
    ro.step4()
    all_received(0, attn_t)

    def send_student(blk, _):
        send_block(blk, 1, mixed_s, attn_s)
        return 0

    lax.fori_loop(0, 8, send_student, 0)
    ro.last()
    ro.end()
    output(attn_t, vel)

    def dh_piece(i, _):
        rows = pl.ds(mult(i * 32, 32), 32)
        clip = i // 2
        xf = x_ref[rows].astype(F32)
        vf = vel[rows].astype(F32)
        rstd = lax.rsqrt(jnp.mean(xf * xf, axis=-1, keepdims=True) + 1e-6)
        cross = jnp.mean(xf * vf, axis=-1, keepdims=True)
        dnormed = rstd * vf - xf * (rstd * rstd * rstd * cross)
        gain = gains[pl.ds(clip * 3 + 1, 1)]
        dgain = gains[pl.ds(clip * 3 + 2, 1)]
        dh[rows] = (dnormed * gain + xf * rstd * dgain).astype(BF16)
        return 0

    lax.fori_loop(0, 4, dh_piece, 0)
    gd = Gather(dh, dg)
    gd.begin()
    all_received(1, attn_s)
    gd.step1()
    gd.step2()
    gd.step3()
    gd.step4()
    output(attn_s, student_ref)
    gd.step5()

    def early_tangent(clip, _):
        base = mult(clip * HALF, BLK)
        project(dg[pl.ds(base, BLK)], base, qkv_d, other_d)
        return 0

    def late_tangent(clip, _):
        base = mult(clip * HALF + BLK, BLK)
        project(dg[pl.ds(base, BLK)], base, qkv_d, other_d)
        return 0

    lax.fori_loop(0, 2, early_tangent, 0)
    swaps_d = [exchange(clip, 0, qkv_d, other_d) for clip in range(2)]
    gd.end_a()
    gd.end_b()
    lax.fori_loop(0, 2, late_tangent, 0)
    swaps_d += [exchange(clip, 1, qkv_d, other_d) for clip in range(2)]
    arrived(*swaps_d)
    lax.fori_loop(0, 8, tangent_block, 0)
    all_received(2, attn_d)
    output(attn_d, tangent_ref)

    for copy in started:
        copy.wait_send()
    for phase, attn in enumerate((attn_t, attn_s, attn_d)):
        all_sent(phase, attn)


def on_device(x_t, clip_len, time_idx, teacher_mod, student_mod, w_qkv, w_out):
    vmem = pl.BlockSpec(memory_space=pltpu.VMEM)
    smem = pl.BlockSpec(memory_space=pltpu.SMEM)
    hbm = pl.BlockSpec(memory_space=pl.ANY)
    rows = CLIPS * SEG
    out = jax.ShapeDtypeStruct((rows, D), BF16)

    def buf(*shape, dtype=BF16):
        return pltpu.VMEM(shape, dtype)

    scratch = [
        buf(CLIPS * HALF, D), buf(CLIPS * HALF, D), buf(D, 768), buf(INNER, D),
        buf(CLIPS * FULL, 384), buf(CLIPS * FULL, 384), buf(CLIPS * FULL, 384),
        buf(CLIPS * HALF, 384), buf(CLIPS * HALF, 384), buf(CLIPS * HALF, 384),
        buf(BLK, D), buf(8, D, dtype=F32), buf(CLIPS * FULL, HD),
        buf(CLIPS * FULL, HD), buf(CLIPS * FULL, HD), buf(CLIPS * FULL, HD),
        buf(rows, INNER), buf(rows, INNER), buf(rows, INNER),
        buf(rows, D), buf(rows, D),
        buf(CLIPS * FULL, FULL, dtype=F32), buf(CLIPS * FULL, FULL),
        pltpu.SemaphoreType.DMA((96,)), pltpu.SemaphoreType.DMA((96,)),
        pltpu.SemaphoreType.DMA((8,)), pltpu.SemaphoreType.DMA((3,)), pltpu.SemaphoreType.DMA((3,)),
    ]
    student, tangent = pl.pallas_call(
        kernel,
        out_shape=(out, out),
        in_specs=[smem, smem, vmem, vmem, vmem, hbm, hbm],
        out_specs=(vmem, vmem),
        scratch_shapes=scratch,
        compiler_params=pltpu.CompilerParams(
            collective_id=0, has_side_effects=True, vmem_limit_bytes=60 * 2**20),
    )(clip_len, time_idx, x_t.reshape(rows, D), teacher_mod, student_mod, w_qkv, w_out)
    return (student.reshape(CLIPS, SEG, D), tangent.reshape(CLIPS, SEG, D))


def solution(mesh):
    in_specs = (
        P("fsdp", "ctx", None), P("fsdp"), P("fsdp"), P(), P(), P("fsdp", None), P("fsdp", None),
    )
    out_specs = (P("fsdp", "ctx", None), P("fsdp", "ctx", None))
    return jax.shard_map(
        on_device, mesh=mesh, in_specs=in_specs, out_specs=out_specs, check_vma=False)
```

```python
import functools
import math

import jax
import jax.numpy as jnp
from jax import lax
from jax.experimental import pallas as pl
from jax.experimental.pallas import tpu as pltpu
from jax.sharding import PartitionSpec as P

HEADS = 16
HD = 128
TIME_STEPS = 1000
D = 1536
INNER = HEADS * HD
SEG = 64
CLIPS = 2
SLOTS = 8
HALF = SLOTS * SEG
FULL = 2 * HALF
BLK = 4 * SEG
SCALE = 1.0 / math.sqrt(HD)
EXP2_SCALE = SCALE * math.log2(math.e)
MESH = pl.DeviceIdType.MESH
F32 = jnp.float32
BF16 = jnp.bfloat16

S00, S01, S03, S10, S02, S11, S13, S12 = range(8)


PLACES = ((0, 0), (0, 1), (0, 3), (1, 0), (0, 2), (1, 1), (1, 3), (1, 2))


def mult(value, by):
    return pl.multiple_of(value, by)


def kernel(
    len_ref, time_ref, x_ref, tmod_ref, smod_ref, wqkv_ref, wout_ref,
    student_ref, tangent_ref,
    xg, dg, wq, wo, qkv_t, qkv_s, qkv_d, other_t, other_s, other_d, h_t, h_s, gains, kmask,
    mixed_t, mixed_s, mixed_d, attn_t, attn_s, attn_d, vel, dh, scaled, weights,
    score0, score1, weigh0, weigh1, total0, total1,
    send, recv, local, bulk_send, bulk_recv,
):
    c = lax.axis_index("ctx")
    f = lax.axis_index("fsdp")
    core = c % 2
    chip = c // 2
    xx = chip % 4
    yl = c // 8
    z = f // 2
    yh = f % 2

    def device(dcore=0, dx=0, dyl=0, dz=0, dyh=0):
        ctx = ((yl + dyl) % 2 * 4 + (xx + dx) % 4) * 2 + (core + dcore) % 2
        return (ctx, (z + dz) % 8 * 2 + (yh + dyh) % 2)

    sibling = device(dcore=1)
    x_up, x_down = device(dx=1), device(dx=3)
    y_in = device(dyl=1)
    y_out = device(dyl=1, dyh=1)
    z_up, z_down = device(dz=1), device(dz=7)

    barrier = pltpu.get_barrier_semaphore()
    partners = [y_out, z_up, z_down]
    for dyl in range(2):
        for dx in range(4):
            for dcore in range(2):
                if dyl + dx + dcore:
                    partners.append(device(dcore=dcore, dx=dx, dyl=dyl))
    for partner in partners:
        pl.semaphore_signal(barrier, inc=1, device_id=partner, device_id_type=MESH)

    used = [0]
    started = []

    def remote(src, dst, where):
        number = used[0]
        used[0] += 1
        copy = pltpu.make_async_remote_copy(
            src_ref=src, dst_ref=dst, send_sem=send.at[number], recv_sem=recv.at[number],
            device_id=where, device_id_type=MESH,
        )
        copy.start()
        started.append(copy)
        return copy

    nlocal = [0]

    def here(src, dst):
        copy = pltpu.make_async_copy(src, dst, local.at[nlocal[0]])
        nlocal[0] += 1
        copy.start()
        return copy

    def arrived(*copies):
        for copy in copies:
            copy.wait_recv()

    class Gather:
        def __init__(self, own, buf):
            self.own, self.buf = own, buf

        def slot(self, clip, slot, lo=0, n=SEG):
            return self.buf.at[pl.ds(clip * HALF + slot * SEG + lo, n)]

        def mine(self, clip):
            return self.own.at[pl.ds(clip * SEG, SEG)]

        def begin(self):
            self.b_up = remote(self.mine(1), self.slot(1, S03), x_up)
            self.b_down = remote(self.mine(1), self.slot(1, S01), x_down)
            self.a_y = remote(self.mine(0), self.slot(0, S10), y_in)
            self.a_up = remote(self.mine(0), self.slot(0, S03), x_up)
            self.a_down = remote(self.mine(0), self.slot(0, S01), x_down)
            self.b_y = remote(self.mine(1), self.slot(1, S10), y_in)
            self.self0 = here(self.mine(0), self.slot(0, S00))
            self.self1 = here(self.mine(1), self.slot(1, S00))

        def step1(self):
            arrived(self.b_up)
            self.b_h_up = remote(self.slot(1, S03, 0, 32), self.slot(1, S02, 0, 32), x_up)
            arrived(self.b_down)
            self.b_h_down = remote(self.slot(1, S01, 32, 32), self.slot(1, S02, 32, 32), x_down)
            self.b_y1 = remote(self.slot(1, S01), self.slot(1, S11), y_in)
            self.b_y3 = remote(self.slot(1, S03), self.slot(1, S13), y_in)

        def step2(self):
            arrived(self.a_y)
            self.a_y_up = remote(self.slot(0, S10), self.slot(0, S13), x_up)
            self.a_y_down = remote(self.slot(0, S10), self.slot(0, S11), x_down)

        def step3(self):
            arrived(self.a_up)
            self.a_h_up = remote(self.slot(0, S03, 0, 32), self.slot(0, S02, 0, 32), x_up)
            arrived(self.a_down)
            self.a_h_down = remote(self.slot(0, S01, 32, 32), self.slot(0, S02, 32, 32), x_down)

        def step4(self):
            arrived(self.b_h_up, self.b_h_down)
            self.b_y2 = remote(self.slot(1, S02), self.slot(1, S12), y_in)
            arrived(self.b_y)
            self.self0.wait()
            self.self1.wait()

        def step5(self):
            arrived(self.a_y_up)
            self.a_yh_up = remote(self.slot(0, S13, 0, 32), self.slot(0, S12, 0, 32), x_up)
            arrived(self.a_y_down)
            self.a_yh_down = remote(self.slot(0, S11, 32, 32), self.slot(0, S12, 32, 32), x_down)

        def end_a(self):
            arrived(self.a_h_up, self.a_h_down, self.a_yh_up, self.a_yh_down)

        def end_b(self):
            arrived(self.b_y1, self.b_y3, self.b_y2)

    class Chain:
        def __init__(self, buf, rows, part, cols, core_cols):
            self.buf, self.rows, self.part = buf, rows, part
            self.cols, self.core_cols = cols, core_cols
            self.cores = []

        def block(self, dz, lo=0, n=None, cols=None):
            base = mult(((z + dz) % 8 * 2 + self.part) * self.rows + lo, 16)
            return self.buf.at[pl.ds(base, n or self.rows), self.cols if cols is None else cols]

        def share(self, dz):
            self.cores.append(remote(
                self.block(dz), self.block(dz, cols=self.core_cols), sibling))

        def step1(self):
            self.up = remote(self.block(0), self.block(0), z_up)
            self.down = remote(self.block(0), self.block(0), z_down)
            self.share(0)

        def step(self, k):
            half = self.rows // 2
            arrived(self.up)
            lo, n = (0, half) if k == 4 else (0, self.rows)
            self.up = remote(self.block(9 - k, lo, n), self.block(9 - k, lo, n), z_up)
            arrived(self.down)
            lo, n = (half, half) if k == 4 else (0, self.rows)
            self.down = remote(self.block(k - 1, lo, n), self.block(k - 1, lo, n), z_down)
            self.share(9 - k)
            self.share(k - 1)

        def last(self):
            arrived(self.up, self.down)
            self.share(4)

        def end(self):
            arrived(*self.cores)

    c_out = (c + 8) % 16
    row_q = mult(f * 96, 16)
    own_q = [
        here(
            wqkv_ref.at[:, pl.ds(mult(part * INNER + c * HD, HD), HD)],
            wq.at[pl.ds(row_q, 96), pl.ds(part * HD, HD)])
        for part in range(3)
    ]
    my_cols = pl.ds(mult(core * 768, HD), 768)
    row_o = mult(f * HD, HD)
    own_o = here(wout_ref.at[:, my_cols], wo.at[pl.ds(row_o, HD), my_cols])
    gx = Gather(x_ref, xg)
    qa = Chain(wq, 96, yh, pl.ds(0, 384), pl.ds(384, 384))
    qb = Chain(wq, 96, 1 - yh, pl.ds(0, 384), pl.ds(384, 384))
    oa = Chain(wo, HD, yh, my_cols, my_cols)
    ob = Chain(wo, HD, 1 - yh, my_cols, my_cols)

    for clip in range(CLIPS):
        angle = jnp.full((1, D), time_ref[clip].astype(F32), F32)
        angle = math.pi / 2 * (angle + 0.5) / TIME_STEPS
        sin_t, cos_t = jnp.sin(angle), jnp.cos(angle)
        gains[pl.ds(clip * 3, 1)] = 1.0 + sin_t * tmod_ref[0:1] + cos_t * tmod_ref[1:2]
        gains[pl.ds(clip * 3 + 1, 1)] = 1.0 + sin_t * smod_ref[0:1] + cos_t * smod_ref[1:2]
        gains[pl.ds(clip * 3 + 2, 1)] = cos_t * smod_ref[0:1] - sin_t * smod_ref[1:2]
    within = lax.broadcasted_iota(jnp.int32, (SEG, HD), 0)
    lane0 = lax.broadcasted_iota(jnp.int32, (SEG, HD), 1) == 0
    for clip in range(CLIPS):
        for half in range(2):
            for slot, (dyl, dx) in enumerate(PLACES):
                token = within + device(dcore=half, dx=dx, dyl=dyl)[0] * SEG
                dead = jnp.logical_and(token >= len_ref[clip], lane0)
                kmask[pl.ds(clip * FULL + half * HALF + slot * SEG, SEG)] = jnp.where(
                    dead, -1e30, 0.0).astype(BF16)
    one0 = jnp.where(lax.broadcasted_iota(jnp.int32, (HALF, HD), 1) == 0, 1.0, 0.0).astype(BF16)

    def project(source, base, out, other):
        y = jnp.dot(source[pl.ds(base, BLK)], wq[...], preferred_element_type=F32).astype(BF16)
        clip, rest = base // HALF, base % HALF
        out[pl.ds(mult(clip * FULL + rest, BLK), BLK)] = y[:, :384]
        other[pl.ds(base, BLK)] = y[:, 384:]

    def modulate(base):
        clip = base // HALF

        def piece(i, _):
            rows = pl.ds(mult(base + i * 32, 32), 32)
            xf = xg[rows].astype(F32)
            rstd = lax.rsqrt(jnp.mean(xf * xf, axis=-1, keepdims=True) + 1e-6)
            normed = xf * rstd
            h_t[rows] = (normed * gains[pl.ds(clip * 3, 1)]).astype(BF16)
            h_s[rows] = (normed * gains[pl.ds(clip * 3 + 1, 1)]).astype(BF16)
            return 0

        lax.fori_loop(0, BLK // 32, piece, 0)

    def exchange(clip, group, out, other):
        return remote(
            other.at[pl.ds(clip * HALF + group * BLK, BLK)],
            out.at[pl.ds(clip * FULL + HALF + group * BLK, BLK)], sibling)

    def send_block(blk, phase, mixed, attn):
        clip, half = blk // 2, blk % 2
        for slot in (7, 4, 5, 6, 3, 1, 2, 0):
            dyl, dx = PLACES[slot]
            src = mixed.at[pl.ds(blk * HALF + slot * SEG, SEG)]
            dst = attn.at[pl.ds(clip * SEG, SEG), pl.ds(mult(c * HD, HD), HD)]
            if half + slot == 0:
                pltpu.make_async_copy(src, dst, bulk_recv.at[phase]).start()
            else:
                pltpu.make_async_remote_copy(
                    src_ref=src, dst_ref=dst, send_sem=bulk_send.at[phase],
                    recv_sem=bulk_recv.at[phase],
                    device_id=device(dcore=half, dx=dx, dyl=dyl), device_id_type=MESH,
                ).start()

    def all_received(phase, attn):
        pltpu.make_async_copy(attn, attn, bulk_recv.at[phase]).wait()

    def all_sent(phase, attn):
        part = attn.at[:, pl.ds(0, INNER - HD)]
        pltpu.make_async_copy(part, part, bulk_send.at[phase]).wait()

    NT = (((1,), (1,)), ((), ()))

    def places_of(blk):
        return pl.ds(blk * HALF, HALF), pl.ds(blk // 2 * FULL, FULL)

    def masked_scores(blk, qkv, out):
        rows, keys = places_of(blk)
        query = jnp.concatenate([qkv[rows, 0:HD], one0], axis=1)
        key = jnp.concatenate([qkv[keys, HD:2 * HD], kmask[keys]], axis=1)
        out[...] = lax.dot_general(query, key, NT, preferred_element_type=F32)

    def pipeline(first, second, third):
        first(0, 0)
        first(1, 1)
        second(0, 0)
        first(2, 0)
        second(1, 1)
        third(0, 0)
        first(3, 1)
        second(2, 0)
        third(1, 1)
        second(3, 1)
        third(2, 0)
        third(3, 1)

    score = (score0, score1)
    weigh = (weigh0, weigh1)
    totals = (total0, total1)

    def teacher_scores(blk, p):
        masked_scores(blk, qkv_t, score[p])

    def teacher_softmax(blk, p):
        scores = score[p][...]
        top = jnp.max(scores, axis=-1, keepdims=True)
        expo = jnp.exp2((scores - top) * EXP2_SCALE)
        totals[p][...] = jnp.broadcast_to(jnp.sum(expo, axis=-1, keepdims=True), (HALF, HD))
        weigh[p][...] = expo.astype(BF16)

    def teacher_values(blk, p):
        rows, keys = places_of(blk)
        out = jnp.dot(weigh[p][...], qkv_t[keys, 2 * HD:], preferred_element_type=F32)
        mixed_t[rows] = (out / totals[p][...]).astype(BF16)
        send_block(blk, 0, mixed_t, attn_t)

    def student_block(blk):
        rows, keys = places_of(blk)
        masked_scores(blk, qkv_s, score[0])
        scores = score[0][...]
        top = jnp.max(scores, axis=-1, keepdims=True)
        expo = jnp.exp2((scores - top) * EXP2_SCALE)
        probs = expo * (1.0 / jnp.sum(expo, axis=-1, keepdims=True))
        weights[rows] = probs.astype(BF16)
        scaled[rows] = probs * SCALE
        mixed_s[rows] = jnp.dot(
            weights[rows], qkv_s[keys, 2 * HD:], preferred_element_type=F32).astype(BF16)

    def tangent_scores(blk, p):
        rows, keys = places_of(blk)
        query = jnp.concatenate([qkv_d[rows, 0:HD], qkv_s[rows, 0:HD]], axis=1)
        key = jnp.concatenate([qkv_s[keys, HD:2 * HD], qkv_d[keys, HD:2 * HD]], axis=1)
        score[p][...] = lax.dot_general(query, key, NT, preferred_element_type=F32)

    def tangent_probs(blk, p):
        rows, keys = places_of(blk)
        dscore = score[p][...]
        prob = scaled[rows]
        mean = jnp.sum(prob * dscore, axis=-1, keepdims=True) * (1.0 / SCALE)
        weigh[p][...] = (prob * (dscore - mean)).astype(BF16)

    def tangent_values(blk, p):
        rows, keys = places_of(blk)
        out = jnp.dot(weigh[p][...], qkv_s[keys, 2 * HD:], preferred_element_type=F32)
        out += jnp.dot(weights[rows], qkv_d[keys, 2 * HD:], preferred_element_type=F32)
        mixed_d[rows] = out.astype(BF16)
        send_block(blk, 2, mixed_d, attn_d)

    def output(attn, out):
        def tile(n, _):
            cols = pl.ds(mult(n * 512, 512), 512)
            out[:, cols] = jnp.dot(
                attn[...], wo[:, cols], preferred_element_type=F32).astype(BF16)
            return 0

        lax.fori_loop(0, 3, tile, 0)

    for copy in own_q:
        copy.wait()
    own_o.wait()
    pl.semaphore_wait(barrier, len(partners))

    qa.step1()
    hop_q = [
        remote(
            wqkv_ref.at[:, pl.ds(mult(part * INNER + c_out * HD, HD), HD)],
            wq.at[pl.ds(row_q, 96), pl.ds(part * HD, HD)], y_out)
        for part in range(3)
    ]
    gx.begin()
    hop_o = remote(wo.at[pl.ds(row_o, HD), my_cols], wo.at[pl.ds(row_o, HD), my_cols], y_out)
    arrived(*hop_q)
    qb.step1()
    qa.step(2)
    gx.step1()
    qb.step(2)
    gx.step2()
    qa.step(3)
    gx.step3()
    qb.step(3)
    qa.step(4)
    oa.step1()
    gx.step4()
    qb.step(4)
    arrived(hop_o)
    ob.step1()
    qa.last()

    modulate(0)
    gx.step5()
    qb.last()
    modulate(HALF)
    oa.step(2)
    qa.end()
    qb.end()
    project(h_t, 0, qkv_t, other_t)
    project(h_t, HALF, qkv_t, other_t)
    swaps_t = [exchange(clip, 0, qkv_t, other_t) for clip in range(2)]
    ob.step(2)
    project(h_s, 0, qkv_s, other_s)
    project(h_s, HALF, qkv_s, other_s)
    swaps_s = [exchange(clip, 0, qkv_s, other_s) for clip in range(2)]
    gx.end_a()
    modulate(BLK)
    project(h_t, BLK, qkv_t, other_t)
    swaps_t.append(exchange(0, 1, qkv_t, other_t))
    oa.step(3)
    gx.end_b()
    modulate(HALF + BLK)
    project(h_t, HALF + BLK, qkv_t, other_t)
    swaps_t.append(exchange(1, 1, qkv_t, other_t))
    project(h_s, BLK, qkv_s, other_s)
    swaps_s.append(exchange(0, 1, qkv_s, other_s))
    arrived(*swaps_t)
    ob.step(3)
    pipeline(teacher_scores, teacher_softmax, teacher_values)
    oa.step(4)
    project(h_s, HALF + BLK, qkv_s, other_s)
    swaps_s.append(exchange(1, 1, qkv_s, other_s))
    ob.step(4)
    all_received(0, attn_t)
    oa.last()
    ob.last()
    oa.end()
    ob.end()
    output(attn_t, vel)

    def dh_piece(i, _):
        rows = pl.ds(mult(i * 32, 32), 32)
        clip = i // 2
        xf = x_ref[rows].astype(F32)
        vf = vel[rows].astype(F32)
        rstd = lax.rsqrt(jnp.mean(xf * xf, axis=-1, keepdims=True) + 1e-6)
        cross = jnp.mean(xf * vf, axis=-1, keepdims=True)
        dnormed = rstd * vf - xf * (rstd * rstd * rstd * cross)
        gain = gains[pl.ds(clip * 3 + 1, 1)]
        dgain = gains[pl.ds(clip * 3 + 2, 1)]
        dh[rows] = (dnormed * gain + xf * rstd * dgain).astype(BF16)
        return 0

    lax.fori_loop(0, 4, dh_piece, 0)
    gd = Gather(dh, dg)
    gd.begin()
    arrived(*swaps_s)
    student_block(0)
    gd.step1()
    gd.step2()
    student_block(1)
    student_block(2)
    gd.step3()
    student_block(3)
    gd.step4()
    gd.step5()
    project(dg, 0, qkv_d, other_d)
    project(dg, HALF, qkv_d, other_d)
    swaps_d = [exchange(clip, 0, qkv_d, other_d) for clip in range(2)]
    gd.end_a()
    project(dg, BLK, qkv_d, other_d)
    swaps_d.append(exchange(0, 1, qkv_d, other_d))
    gd.end_b()
    project(dg, HALF + BLK, qkv_d, other_d)
    swaps_d.append(exchange(1, 1, qkv_d, other_d))
    for blk in range(4):
        send_block(blk, 1, mixed_s, attn_s)
    arrived(*swaps_d)
    pipeline(tangent_scores, tangent_probs, tangent_values)
    all_received(1, attn_s)
    output(attn_s, student_ref)
    all_received(2, attn_d)
    output(attn_d, tangent_ref)

    for copy in started:
        copy.wait_send()
    for phase, attn in enumerate((attn_t, attn_s, attn_d)):
        all_sent(phase, attn)


def on_device(x_t, clip_len, time_idx, teacher_mod, student_mod, w_qkv, w_out):
    vmem = pl.BlockSpec(memory_space=pltpu.VMEM)
    smem = pl.BlockSpec(memory_space=pltpu.SMEM)
    hbm = pl.BlockSpec(memory_space=pl.ANY)
    rows = CLIPS * SEG
    out = jax.ShapeDtypeStruct((rows, D), BF16)

    def buf(*shape, dtype=BF16):
        return pltpu.VMEM(shape, dtype)

    scratch = [
        buf(CLIPS * HALF, D), buf(CLIPS * HALF, D), buf(D, 768), buf(INNER, D),
        buf(CLIPS * FULL, 384), buf(CLIPS * FULL, 384), buf(CLIPS * FULL, 384),
        buf(CLIPS * HALF, 384), buf(CLIPS * HALF, 384), buf(CLIPS * HALF, 384),
        buf(CLIPS * HALF, D), buf(CLIPS * HALF, D), buf(8, D, dtype=F32), buf(CLIPS * FULL, HD),
        buf(CLIPS * FULL, HD), buf(CLIPS * FULL, HD), buf(CLIPS * FULL, HD),
        buf(rows, INNER), buf(rows, INNER), buf(rows, INNER),
        buf(rows, D), buf(rows, D),
        buf(CLIPS * FULL, FULL, dtype=F32), buf(CLIPS * FULL, FULL),
        buf(HALF, FULL, dtype=F32), buf(HALF, FULL, dtype=F32), buf(HALF, FULL), buf(HALF, FULL),
        buf(HALF, HD, dtype=F32), buf(HALF, HD, dtype=F32),
        pltpu.SemaphoreType.DMA((128,)), pltpu.SemaphoreType.DMA((128,)),
        pltpu.SemaphoreType.DMA((8,)), pltpu.SemaphoreType.DMA((3,)), pltpu.SemaphoreType.DMA((3,)),
    ]
    student, tangent = pl.pallas_call(
        kernel,
        out_shape=(out, out),
        in_specs=[smem, smem, vmem, vmem, vmem, hbm, hbm],
        out_specs=(vmem, vmem),
        scratch_shapes=scratch,
        compiler_params=pltpu.CompilerParams(
            collective_id=0, has_side_effects=True, vmem_limit_bytes=60 * 2**20),
    )(clip_len, time_idx, x_t.reshape(rows, D), teacher_mod, student_mod, w_qkv, w_out)
    return (student.reshape(CLIPS, SEG, D), tangent.reshape(CLIPS, SEG, D))


def solution(mesh):
    in_specs = (
        P("fsdp", "ctx", None), P("fsdp"), P("fsdp"), P(), P(), P("fsdp", None), P("fsdp", None),
    )
    out_specs = (P("fsdp", "ctx", None), P("fsdp", "ctx", None))
    return jax.shard_map(
        on_device, mesh=mesh, in_specs=in_specs, out_specs=out_specs, check_vma=False)
```

```python
import functools
import math

import jax
import jax.numpy as jnp
from jax import lax
from jax.experimental import pallas as pl
from jax.experimental.pallas import tpu as pltpu
from jax.sharding import PartitionSpec as P

HEADS = 16
HD = 128
TIME_STEPS = 1000
D = 1536
INNER = HEADS * HD
SEG = 64
CLIPS = 2
SLOTS = 8
HALF = SLOTS * SEG
FULL = 2 * HALF
BLK = 4 * SEG
SCALE = 1.0 / math.sqrt(HD)
EXP2_SCALE = SCALE * math.log2(math.e)
MESH = pl.DeviceIdType.MESH
F32 = jnp.float32
BF16 = jnp.bfloat16

RING = 256

S00, S01, S03, S10, S02, S11, S13, S12 = range(8)


PLACES = ((0, 0), (0, 1), (0, 3), (1, 0), (0, 2), (1, 1), (1, 3), (1, 2))


def mult(value, by):
    return pl.multiple_of(value, by)


def kernel(
    len_ref, time_ref, x_ref, tmod_ref, smod_ref, wqkv_ref, wout_ref,
    student_ref, tangent_ref,
    xg, dg, wq, wo, qkv_t, qkv_s, qkv_d, other_t, other_s, other_d, h_t, h_s, gains, kmask,
    mixed_t, mixed_s, mixed_d, attn_t, attn_s, attn_d, vel, dh, scaled, weights,
    score0, score1, weigh0, weigh1, total0, total1,
    send, recv, local, bulk_send, bulk_recv,
):
    c = lax.axis_index("ctx")
    f = lax.axis_index("fsdp")
    core = c % 2
    chip = c // 2
    xx = chip % 4
    yl = c // 8
    z = f // 2
    yh = f % 2

    chips = [((yl + dyl) % 2 * 4 + (xx + dx) % 4) * 2 for dyl, dx in PLACES]
    halves = (core, 1 - core)
    columns = [(z + dz) % 8 * 2 for dz in range(8)]

    def member(slot, half):
        return chips[slot] + halves[half]

    sibling = (member(S00, 1), f)
    x_up, x_down = (member(S01, 0), f), (member(S03, 0), f)
    y_in = (member(S10, 0), f)
    y_out = (member(S10, 0), columns[0] + 1 - yh)
    z_up, z_down = (c, columns[1] + yh), (c, columns[7] + yh)

    barrier = pltpu.get_barrier_semaphore()
    partners = [y_out, z_up, z_down]
    for slot in range(SLOTS):
        for half in range(2):
            if slot + half:
                partners.append((member(slot, half), f))
    for partner in partners:
        pl.semaphore_signal(barrier, inc=1, device_id=partner, device_id_type=MESH)

    used = [0]
    started = []

    def remote(src, dst, where):
        number = used[0]
        used[0] += 1
        copy = pltpu.make_async_remote_copy(
            src_ref=src, dst_ref=dst, send_sem=send.at[number], recv_sem=recv.at[number],
            device_id=where, device_id_type=MESH,
        )
        copy.start()
        started.append(copy)
        return copy

    nlocal = [0]

    def here(src, dst):
        copy = pltpu.make_async_copy(src, dst, local.at[nlocal[0]])
        nlocal[0] += 1
        copy.start()
        return copy

    def arrived(*copies):
        for copy in copies:
            copy.wait_recv()

    class Gather:
        def __init__(self, own, buf):
            self.own, self.buf = own, buf

        def slot(self, clip, slot, lo=0, n=SEG):
            return self.buf.at[pl.ds(clip * HALF + slot * SEG + lo, n)]

        def mine(self, clip):
            return self.own.at[pl.ds(clip * SEG, SEG)]

        def begin(self):
            self.b_up = remote(self.mine(1), self.slot(1, S03), x_up)
            self.b_down = remote(self.mine(1), self.slot(1, S01), x_down)
            self.a_y = remote(self.mine(0), self.slot(0, S10), y_in)
            self.a_up = remote(self.mine(0), self.slot(0, S03), x_up)
            self.a_down = remote(self.mine(0), self.slot(0, S01), x_down)
            self.b_y = remote(self.mine(1), self.slot(1, S10), y_in)
            self.self0 = here(self.mine(0), self.slot(0, S00))
            self.self1 = here(self.mine(1), self.slot(1, S00))

        def step1(self):
            arrived(self.b_up)
            self.b_h_up = remote(self.slot(1, S03, 0, 32), self.slot(1, S02, 0, 32), x_up)
            arrived(self.b_down)
            self.b_h_down = remote(self.slot(1, S01, 32, 32), self.slot(1, S02, 32, 32), x_down)
            self.b_y1 = remote(self.slot(1, S01), self.slot(1, S11), y_in)
            self.b_y3 = remote(self.slot(1, S03), self.slot(1, S13), y_in)

        def step2(self):
            arrived(self.a_y)
            self.a_y_up = remote(self.slot(0, S10), self.slot(0, S13), x_up)
            self.a_y_down = remote(self.slot(0, S10), self.slot(0, S11), x_down)

        def step3(self):
            arrived(self.a_up)
            self.a_h_up = remote(self.slot(0, S03, 0, 32), self.slot(0, S02, 0, 32), x_up)
            arrived(self.a_down)
            self.a_h_down = remote(self.slot(0, S01, 32, 32), self.slot(0, S02, 32, 32), x_down)

        def step4(self):
            arrived(self.b_h_up, self.b_h_down)
            self.b_y2 = remote(self.slot(1, S02), self.slot(1, S12), y_in)
            arrived(self.b_y)
            self.self0.wait()
            self.self1.wait()

        def step5(self):
            arrived(self.a_y_up)
            self.a_yh_up = remote(self.slot(0, S13, 0, 32), self.slot(0, S12, 0, 32), x_up)
            arrived(self.a_y_down)
            self.a_yh_down = remote(self.slot(0, S11, 32, 32), self.slot(0, S12, 32, 32), x_down)

        def end_a(self):
            arrived(self.a_h_up, self.a_h_down, self.a_yh_up, self.a_yh_down)

        def end_b(self):
            arrived(self.b_y1, self.b_y3, self.b_y2)

    class Chain:
        def __init__(self, buf, rows, part, cols, core_cols, first=0, count=None):
            self.buf, self.rows, self.part = buf, rows, part
            self.first, self.count = first, count or rows
            self.cols, self.core_cols = cols, core_cols
            self.cores = []

        def block(self, dz, lo=0, n=None, cols=None, part=None):
            at = columns[dz % 8] + (self.part if part is None else part)
            base = mult(at * self.rows + self.first + lo, 16)
            return self.buf.at[pl.ds(base, n or self.count), self.cols if cols is None else cols]

        def share(self, dz):
            self.cores.append(remote(
                self.block(dz), self.block(dz, cols=self.core_cols), sibling))

        def step1(self):
            self.up = remote(self.block(0), self.block(0), z_up)
            self.down = remote(self.block(0), self.block(0), z_down)
            self.share(0)

        def step(self, k):
            half = self.count // 2
            arrived(self.up)
            lo, n = (0, half) if k == 4 else (0, self.count)
            self.up = remote(self.block(9 - k, lo, n), self.block(9 - k, lo, n), z_up)
            arrived(self.down)
            lo, n = (half, half) if k == 4 else (0, self.count)
            self.down = remote(self.block(k - 1, lo, n), self.block(k - 1, lo, n), z_down)
            self.share(9 - k)
            self.share(k - 1)

        def last(self):
            arrived(self.up, self.down)
            self.share(4)

        def end(self):
            arrived(*self.cores)

    class WideChain(Chain):
        def __init__(self, across_cols, *args):
            super().__init__(*args)
            self.across_cols, self.across = across_cols, []

        def share(self, dz):
            across = self.block(dz, cols=self.across_cols)
            self.across.append((dz, remote(across, across, y_out)))
            super().share(dz)

        def take(self, leave=0):
            while len(self.across) > leave:
                dz, copy = self.across.pop(0)
                arrived(copy)
                there = self.block(dz, cols=self.across_cols, part=1 - self.part)
                self.cores.append(remote(there, there, sibling))

    c_out = (c + 8) % 16
    row_q = mult(f * 96, 16)
    own_q = [
        here(
            wqkv_ref.at[:, pl.ds(mult(part * INNER + c * HD, HD), HD)],
            wq.at[pl.ds(row_q, 96), pl.ds(part * HD, HD)])
        for part in range(3)
    ]
    my_cols = pl.ds(mult(core * 768, HD), 768)
    row_o = mult(f * HD, HD)
    own_o = here(wout_ref.at[:, my_cols], wo.at[pl.ds(row_o, HD), my_cols])
    gx = Gather(x_ref, xg)
    qa = Chain(wq, 96, yh, pl.ds(0, 384), pl.ds(384, 384))
    qb = Chain(wq, 96, 1 - yh, pl.ds(0, 384), pl.ds(384, 384))
    ring_cols = pl.ds(mult(core * 768, HD), RING)
    across_cols = pl.ds(mult(core * 768 + RING, HD), 768 - RING)
    oa = WideChain(across_cols, wo, HD, yh, my_cols, my_cols, 0, 64)
    oc = WideChain(across_cols, wo, HD, yh, my_cols, my_cols, 64, 64)
    ob = Chain(wo, HD, 1 - yh, ring_cols, ring_cols)

    for clip in range(CLIPS):
        angle = jnp.full((1, D), time_ref[clip].astype(F32), F32)
        angle = math.pi / 2 * (angle + 0.5) / TIME_STEPS
        sin_t, cos_t = jnp.sin(angle), jnp.cos(angle)
        gains[pl.ds(clip * 3, 1)] = 1.0 + sin_t * tmod_ref[0:1] + cos_t * tmod_ref[1:2]
        gains[pl.ds(clip * 3 + 1, 1)] = 1.0 + sin_t * smod_ref[0:1] + cos_t * smod_ref[1:2]
        gains[pl.ds(clip * 3 + 2, 1)] = cos_t * smod_ref[0:1] - sin_t * smod_ref[1:2]
    within = lax.broadcasted_iota(jnp.int32, (SEG, HD), 0)
    lane0 = lax.broadcasted_iota(jnp.int32, (SEG, HD), 1) == 0
    for clip in range(CLIPS):
        for half in range(2):
            for slot in range(SLOTS):
                token = within + member(slot, half) * SEG
                dead = jnp.logical_and(token >= len_ref[clip], lane0)
                kmask[pl.ds(clip * FULL + half * HALF + slot * SEG, SEG)] = jnp.where(
                    dead, -1e30, 0.0).astype(BF16)
    one0 = jnp.where(lax.broadcasted_iota(jnp.int32, (HALF, HD), 1) == 0, 1.0, 0.0).astype(BF16)

    def project(source, base, out, other):
        y = jnp.dot(source[pl.ds(base, BLK)], wq[...], preferred_element_type=F32).astype(BF16)
        clip, rest = base // HALF, base % HALF
        out[pl.ds(mult(clip * FULL + rest, BLK), BLK)] = y[:, :384]
        other[pl.ds(base, BLK)] = y[:, 384:]

    def modulate(base):
        clip = base // HALF

        def piece(i, _):
            rows = pl.ds(mult(base + i * 32, 32), 32)
            xf = xg[rows].astype(F32)
            rstd = lax.rsqrt(jnp.mean(xf * xf, axis=-1, keepdims=True) + 1e-6)
            normed = xf * rstd
            h_t[rows] = (normed * gains[pl.ds(clip * 3, 1)]).astype(BF16)
            h_s[rows] = (normed * gains[pl.ds(clip * 3 + 1, 1)]).astype(BF16)
            return 0

        lax.fori_loop(0, BLK // 32, piece, 0)

    def exchange(clip, group, out, other):
        return remote(
            other.at[pl.ds(clip * HALF + group * BLK, BLK)],
            out.at[pl.ds(clip * FULL + HALF + group * BLK, BLK)], sibling)

    def send_block(blk, phase, mixed, attn):
        clip, half = blk // 2, blk % 2
        for slot in (7, 4, 5, 6, 3, 1, 2, 0):
            src = mixed.at[pl.ds(blk * HALF + slot * SEG, SEG)]
            dst = attn.at[pl.ds(clip * SEG, SEG), pl.ds(mult(c * HD, HD), HD)]
            if half + slot == 0:
                pltpu.make_async_copy(src, dst, bulk_recv.at[phase]).start()
            else:
                pltpu.make_async_remote_copy(
                    src_ref=src, dst_ref=dst, send_sem=bulk_send.at[phase],
                    recv_sem=bulk_recv.at[phase],
                    device_id=(member(slot, half), f), device_id_type=MESH,
                ).start()

    def all_received(phase, attn):
        pltpu.make_async_copy(attn, attn, bulk_recv.at[phase]).wait()

    def all_sent(phase, attn):
        part = attn.at[:, pl.ds(0, INNER - HD)]
        pltpu.make_async_copy(part, part, bulk_send.at[phase]).wait()

    NT = (((1,), (1,)), ((), ()))

    def places_of(blk):
        return pl.ds(blk * HALF, HALF), pl.ds(blk // 2 * FULL, FULL)

    def masked_scores(blk, qkv, out):
        rows, keys = places_of(blk)
        query = jnp.concatenate([qkv[rows, 0:HD], one0], axis=1)
        key = jnp.concatenate([qkv[keys, HD:2 * HD], kmask[keys]], axis=1)
        out[...] = lax.dot_general(query, key, NT, preferred_element_type=F32)

    def pipeline(first, second, third, between=lambda stage: None):
        first(0, 0)
        first(1, 1)
        second(0, 0)
        first(2, 0)
        second(1, 1)
        third(0, 0)
        between(0)
        first(3, 1)
        second(2, 0)
        third(1, 1)
        between(1)
        second(3, 1)
        third(2, 0)
        third(3, 1)

    score = (score0, score1)
    weigh = (weigh0, weigh1)
    totals = (total0, total1)

    def teacher_scores(blk, p):
        masked_scores(blk, qkv_t, score[p])

    def teacher_softmax(blk, p):
        scores = score[p][...]
        top = jnp.max(scores, axis=-1, keepdims=True)
        expo = jnp.exp2((scores - top) * EXP2_SCALE)
        totals[p][...] = jnp.broadcast_to(jnp.sum(expo, axis=-1, keepdims=True), (HALF, HD))
        weigh[p][...] = expo.astype(BF16)

    def teacher_values(blk, p):
        rows, keys = places_of(blk)
        out = jnp.dot(weigh[p][...], qkv_t[keys, 2 * HD:], preferred_element_type=F32)
        mixed_t[rows] = (out / totals[p][...]).astype(BF16)
        send_block(blk, 0, mixed_t, attn_t)

    def student_block(blk):
        rows, keys = places_of(blk)
        masked_scores(blk, qkv_s, score[0])
        scores = score[0][...]
        top = jnp.max(scores, axis=-1, keepdims=True)
        expo = jnp.exp2((scores - top) * EXP2_SCALE)
        probs = expo * (1.0 / jnp.sum(expo, axis=-1, keepdims=True))
        weights[rows] = probs.astype(BF16)
        scaled[rows] = probs * SCALE
        mixed_s[rows] = jnp.dot(
            weights[rows], qkv_s[keys, 2 * HD:], preferred_element_type=F32).astype(BF16)

    def tangent_scores(blk, p):
        rows, keys = places_of(blk)
        query = jnp.concatenate([qkv_d[rows, 0:HD], qkv_s[rows, 0:HD]], axis=1)
        key = jnp.concatenate([qkv_s[keys, HD:2 * HD], qkv_d[keys, HD:2 * HD]], axis=1)
        score[p][...] = lax.dot_general(query, key, NT, preferred_element_type=F32)

    def tangent_probs(blk, p):
        rows, keys = places_of(blk)
        dscore = score[p][...]
        prob = scaled[rows]
        mean = jnp.sum(prob * dscore, axis=-1, keepdims=True) * (1.0 / SCALE)
        weigh[p][...] = (prob * (dscore - mean)).astype(BF16)

    def tangent_values(blk, p):
        rows, keys = places_of(blk)
        out = jnp.dot(weigh[p][...], qkv_s[keys, 2 * HD:], preferred_element_type=F32)
        out += jnp.dot(weights[rows], qkv_d[keys, 2 * HD:], preferred_element_type=F32)
        mixed_d[rows] = out.astype(BF16)
        send_block(blk, 2, mixed_d, attn_d)

    def output(attn, out):
        def tile(n, _):
            cols = pl.ds(mult(n * 512, 512), 512)
            out[:, cols] = jnp.dot(
                attn[...], wo[:, cols], preferred_element_type=F32).astype(BF16)
            return 0

        lax.fori_loop(0, 3, tile, 0)

    for copy in own_q:
        copy.wait()
    own_o.wait()
    pl.semaphore_wait(barrier, len(partners))

    qa.step1()
    hop_q = [
        remote(
            wqkv_ref.at[:, pl.ds(mult(part * INNER + c_out * HD, HD), HD)],
            wq.at[pl.ds(row_q, 96), pl.ds(part * HD, HD)], y_out)
        for part in range(3)
    ]
    gx.begin()
    arrived(*hop_q)
    qb.step1()
    qa.step(2)
    gx.step1()
    gx.step2()
    qb.step(2)
    hop_o = remote(
        wo.at[pl.ds(row_o, HD), ring_cols], wo.at[pl.ds(row_o, HD), ring_cols], y_out)
    qa.step(3)
    oa.step1()
    gx.step3()
    qb.step(3)
    oc.step1()
    gx.step4()
    qa.step(4)
    arrived(hop_o)
    ob.step1()
    qb.step(4)
    gx.step5()
    modulate(0)
    qa.last()
    modulate(HALF)
    qb.last()
    oa.step(2)
    oc.step(2)
    qa.end()
    qb.end()

    project(h_t, 0, qkv_t, other_t)
    project(h_t, HALF, qkv_t, other_t)
    swaps_t = [exchange(clip, 0, qkv_t, other_t) for clip in range(2)]
    ob.step(2)
    gx.end_a()
    modulate(BLK)
    project(h_t, BLK, qkv_t, other_t)
    swaps_t.append(exchange(0, 1, qkv_t, other_t))
    gx.end_b()
    modulate(HALF + BLK)
    project(h_t, HALF + BLK, qkv_t, other_t)
    swaps_t.append(exchange(1, 1, qkv_t, other_t))
    oa.step(3)
    oc.step(3)
    project(h_s, 0, qkv_s, other_s)
    swaps_s = [exchange(0, 0, qkv_s, other_s)]
    arrived(*swaps_t)

    def between(stage):
        if stage == 0:
            ob.step(3)
            oa.step(4)
        if stage == 1:
            oc.step(4)

    pipeline(teacher_scores, teacher_softmax, teacher_values, between)
    ob.step(4)
    project(h_s, HALF, qkv_s, other_s)
    swaps_s.append(exchange(1, 0, qkv_s, other_s))
    oa.last()
    project(h_s, BLK, qkv_s, other_s)
    oc.last()
    project(h_s, HALF + BLK, qkv_s, other_s)
    swaps_s += [exchange(clip, 1, qkv_s, other_s) for clip in range(2)]
    ob.last()
    oa.take()
    oc.take()
    all_received(0, attn_t)
    oa.end()
    oc.end()
    ob.end()
    output(attn_t, vel)

    def dh_piece(i, _):
        rows = pl.ds(mult(i * 32, 32), 32)
        clip = i // 2
        xf = x_ref[rows].astype(F32)
        vf = vel[rows].astype(F32)
        rstd = lax.rsqrt(jnp.mean(xf * xf, axis=-1, keepdims=True) + 1e-6)
        cross = jnp.mean(xf * vf, axis=-1, keepdims=True)
        dnormed = rstd * vf - xf * (rstd * rstd * rstd * cross)
        gain = gains[pl.ds(clip * 3 + 1, 1)]
        dgain = gains[pl.ds(clip * 3 + 2, 1)]
        dh[rows] = (dnormed * gain + xf * rstd * dgain).astype(BF16)
        return 0

    lax.fori_loop(0, 4, dh_piece, 0)
    gd = Gather(dh, dg)
    gd.begin()
    arrived(*swaps_s)
    student_block(0)
    gd.step1()
    gd.step2()
    student_block(1)
    student_block(2)
    gd.step3()
    student_block(3)
    gd.step4()
    gd.step5()
    project(dg, 0, qkv_d, other_d)
    project(dg, HALF, qkv_d, other_d)
    swaps_d = [exchange(clip, 0, qkv_d, other_d) for clip in range(2)]
    gd.end_a()
    project(dg, BLK, qkv_d, other_d)
    swaps_d.append(exchange(0, 1, qkv_d, other_d))
    gd.end_b()
    project(dg, HALF + BLK, qkv_d, other_d)
    swaps_d.append(exchange(1, 1, qkv_d, other_d))
    for blk in range(4):
        send_block(blk, 1, mixed_s, attn_s)
    arrived(*swaps_d)
    pipeline(tangent_scores, tangent_probs, tangent_values)
    all_received(1, attn_s)
    output(attn_s, student_ref)
    all_received(2, attn_d)
    output(attn_d, tangent_ref)

    for copy in started:
        copy.wait_send()
    for phase, attn in enumerate((attn_t, attn_s, attn_d)):
        all_sent(phase, attn)


def hand_over(student_ref, tangent_ref, student_out, tangent_out):
    student_out[...] = student_ref[...]
    tangent_out[...] = tangent_ref[...]


def on_device(x_t, clip_len, time_idx, teacher_mod, student_mod, w_qkv, w_out):
    vmem = pl.BlockSpec(memory_space=pltpu.VMEM)
    smem = pl.BlockSpec(memory_space=pltpu.SMEM)
    hbm = pl.BlockSpec(memory_space=pl.ANY)
    rows = CLIPS * SEG
    out = jax.ShapeDtypeStruct((rows, D), BF16)

    def buf(*shape, dtype=BF16):
        return pltpu.VMEM(shape, dtype)

    scratch = [
        buf(CLIPS * HALF, D), buf(CLIPS * HALF, D), buf(D, 768), buf(INNER, D),
        buf(CLIPS * FULL, 384), buf(CLIPS * FULL, 384), buf(CLIPS * FULL, 384),
        buf(CLIPS * HALF, 384), buf(CLIPS * HALF, 384), buf(CLIPS * HALF, 384),
        buf(CLIPS * HALF, D), buf(CLIPS * HALF, D), buf(8, D, dtype=F32), buf(CLIPS * FULL, HD),
        buf(CLIPS * FULL, HD), buf(CLIPS * FULL, HD), buf(CLIPS * FULL, HD),
        buf(rows, INNER), buf(rows, INNER), buf(rows, INNER),
        buf(rows, D), buf(rows, D),
        buf(CLIPS * FULL, FULL, dtype=F32), buf(CLIPS * FULL, FULL),
        buf(HALF, FULL, dtype=F32), buf(HALF, FULL, dtype=F32), buf(HALF, FULL), buf(HALF, FULL),
        buf(HALF, HD, dtype=F32), buf(HALF, HD, dtype=F32),
        pltpu.SemaphoreType.DMA((192,)), pltpu.SemaphoreType.DMA((192,)),
        pltpu.SemaphoreType.DMA((8,)), pltpu.SemaphoreType.DMA((3,)), pltpu.SemaphoreType.DMA((3,)),
    ]
    student, tangent = pl.pallas_call(
        kernel,
        out_shape=(out, out),
        in_specs=[smem, smem, vmem, vmem, vmem, hbm, hbm],
        out_specs=(vmem, vmem),
        scratch_shapes=scratch,
        compiler_params=pltpu.CompilerParams(
            collective_id=0, has_side_effects=True, vmem_limit_bytes=60 * 2**20),
    )(clip_len, time_idx, x_t.reshape(rows, D), teacher_mod, student_mod, w_qkv, w_out)
    student, tangent = pl.pallas_call(
        hand_over,
        out_shape=(out, out),
        in_specs=[vmem, vmem],
        out_specs=(vmem, vmem),
    )(student, tangent)
    return (student.reshape(CLIPS, SEG, D), tangent.reshape(CLIPS, SEG, D))


def solution(mesh):
    in_specs = (
        P("fsdp", "ctx", None), P("fsdp"), P("fsdp"), P(), P(), P("fsdp", None), P("fsdp", None),
    )
    out_specs = (P("fsdp", "ctx", None), P("fsdp", "ctx", None))
    return jax.shard_map(
        on_device, mesh=mesh, in_specs=in_specs, out_specs=out_specs, check_vma=False)
```

```python
import functools
import math

import jax
import jax.numpy as jnp
from jax import lax
from jax.experimental import pallas as pl
from jax.experimental.pallas import tpu as pltpu
from jax.sharding import PartitionSpec as P

HEADS = 16
HD = 128
TIME_STEPS = 1000
D = 1536
INNER = HEADS * HD
SEG = 64
CLIPS = 2
SLOTS = 8
HALF = SLOTS * SEG
FULL = 2 * HALF
BLK = 4 * SEG
SCALE = 1.0 / math.sqrt(HD)
EXP2_SCALE = SCALE * math.log2(math.e)
MESH = pl.DeviceIdType.MESH
F32 = jnp.float32
BF16 = jnp.bfloat16

RING = 256

S00, S01, S03, S10, S02, S11, S13, S12 = range(8)


PLACES = ((0, 0), (0, 1), (0, 3), (1, 0), (0, 2), (1, 1), (1, 3), (1, 2))


def mult(value, by):
    return pl.multiple_of(value, by)


def kernel(
    len_ref, time_ref, x_ref, tmod_ref, smod_ref, wqkv_ref, wout_ref,
    student_ref, tangent_ref,
    xg, dg, wq, wo, qkv_t, qkv_s, qkv_d, other_t, other_s, other_d, h_t, h_s, gains, kmask,
    mixed_t, mixed_s, mixed_d, attn_t, attn_s, attn_d, vel, dh, scaled, weights,
    score0, score1, weigh0, weigh1, total0, total1,
    send, recv, local, bulk_send, bulk_recv,
):
    c = lax.axis_index("ctx")
    f = lax.axis_index("fsdp")
    core = c % 2
    chip = c // 2
    xx = chip % 4
    yl = c // 8
    z = f // 2
    yh = f % 2

    chips = [((yl + dyl) % 2 * 4 + (xx + dx) % 4) * 2 for dyl, dx in PLACES]
    halves = (core, 1 - core)
    columns = [(z + dz) % 8 * 2 for dz in range(8)]

    def member(slot, half):
        return chips[slot] + halves[half]

    sibling = (member(S00, 1), f)
    x_up, x_down = (member(S01, 0), f), (member(S03, 0), f)
    y_in = (member(S10, 0), f)
    y_out = (member(S10, 0), columns[0] + 1 - yh)
    z_up, z_down = (c, columns[1] + yh), (c, columns[7] + yh)

    barrier = pltpu.get_barrier_semaphore()
    partners = [y_out, z_up, z_down]
    for slot in range(SLOTS):
        for half in range(2):
            if slot + half:
                partners.append((member(slot, half), f))
    for partner in partners:
        pl.semaphore_signal(barrier, inc=1, device_id=partner, device_id_type=MESH)

    used = [0]
    started = []

    def remote(src, dst, where):
        number = used[0]
        used[0] += 1
        copy = pltpu.make_async_remote_copy(
            src_ref=src, dst_ref=dst, send_sem=send.at[number], recv_sem=recv.at[number],
            device_id=where, device_id_type=MESH,
        )
        copy.start()
        started.append(copy)
        return copy

    nlocal = [0]

    def here(src, dst):
        copy = pltpu.make_async_copy(src, dst, local.at[nlocal[0]])
        nlocal[0] += 1
        copy.start()
        return copy

    def arrived(*copies):
        for copy in copies:
            copy.wait_recv()

    class Gather:
        def __init__(self, own, buf):
            self.own, self.buf = own, buf

        def slot(self, clip, slot, lo=0, n=SEG):
            return self.buf.at[pl.ds(clip * HALF + slot * SEG + lo, n)]

        def mine(self, clip):
            return self.own.at[pl.ds(clip * SEG, SEG)]

        def begin(self):
            self.b_up = remote(self.mine(1), self.slot(1, S03), x_up)
            self.b_down = remote(self.mine(1), self.slot(1, S01), x_down)
            self.a_y = remote(self.mine(0), self.slot(0, S10), y_in)
            self.a_up = remote(self.mine(0), self.slot(0, S03), x_up)
            self.a_down = remote(self.mine(0), self.slot(0, S01), x_down)
            self.b_y = remote(self.mine(1), self.slot(1, S10), y_in)
            self.self0 = here(self.mine(0), self.slot(0, S00))
            self.self1 = here(self.mine(1), self.slot(1, S00))

        def step1(self):
            arrived(self.b_up)
            self.b_h_up = remote(self.slot(1, S03, 0, 32), self.slot(1, S02, 0, 32), x_up)
            arrived(self.b_down)
            self.b_h_down = remote(self.slot(1, S01, 32, 32), self.slot(1, S02, 32, 32), x_down)
            self.b_y1 = remote(self.slot(1, S01), self.slot(1, S11), y_in)
            self.b_y3 = remote(self.slot(1, S03), self.slot(1, S13), y_in)

        def step2(self):
            arrived(self.a_y)
            self.a_y_up = remote(self.slot(0, S10), self.slot(0, S13), x_up)
            self.a_y_down = remote(self.slot(0, S10), self.slot(0, S11), x_down)

        def step3(self):
            arrived(self.a_up)
            self.a_h_up = remote(self.slot(0, S03, 0, 32), self.slot(0, S02, 0, 32), x_up)
            arrived(self.a_down)
            self.a_h_down = remote(self.slot(0, S01, 32, 32), self.slot(0, S02, 32, 32), x_down)

        def step4(self):
            arrived(self.b_h_up, self.b_h_down)
            self.b_y2 = remote(self.slot(1, S02), self.slot(1, S12), y_in)
            arrived(self.b_y)
            self.self0.wait()
            self.self1.wait()

        def step5(self):
            arrived(self.a_y_up)
            self.a_yh_up = remote(self.slot(0, S13, 0, 32), self.slot(0, S12, 0, 32), x_up)
            arrived(self.a_y_down)
            self.a_yh_down = remote(self.slot(0, S11, 32, 32), self.slot(0, S12, 32, 32), x_down)

        def end_a(self):
            arrived(self.a_h_up, self.a_h_down, self.a_yh_up, self.a_yh_down)

        def end_b(self):
            arrived(self.b_y1, self.b_y3, self.b_y2)

    class Chain:
        def __init__(self, buf, rows, part, cols, core_cols, first=0, count=None):
            self.buf, self.rows, self.part = buf, rows, part
            self.first, self.count = first, count or rows
            self.cols, self.core_cols = cols, core_cols
            self.cores = []

        def block(self, dz, lo=0, n=None, cols=None, part=None):
            at = columns[dz % 8] + (self.part if part is None else part)
            base = mult(at * self.rows + self.first + lo, 16)
            return self.buf.at[pl.ds(base, n or self.count), self.cols if cols is None else cols]

        def share(self, dz):
            self.cores.append(remote(
                self.block(dz), self.block(dz, cols=self.core_cols), sibling))

        def step1(self):
            self.up = remote(self.block(0), self.block(0), z_up)
            self.down = remote(self.block(0), self.block(0), z_down)
            self.share(0)

        def step(self, k):
            half = self.count // 2
            arrived(self.up)
            lo, n = (0, half) if k == 4 else (0, self.count)
            self.up = remote(self.block(9 - k, lo, n), self.block(9 - k, lo, n), z_up)
            arrived(self.down)
            lo, n = (half, half) if k == 4 else (0, self.count)
            self.down = remote(self.block(k - 1, lo, n), self.block(k - 1, lo, n), z_down)
            self.share(9 - k)
            self.share(k - 1)

        def last(self):
            arrived(self.up, self.down)
            self.share(4)

        def end(self):
            arrived(*self.cores)

    class WideChain(Chain):
        def __init__(self, across_cols, *args):
            super().__init__(*args)
            self.across_cols, self.across = across_cols, []

        def share(self, dz):
            across = self.block(dz, cols=self.across_cols)
            self.across.append((dz, remote(across, across, y_out)))
            super().share(dz)

        def take(self, leave=0):
            while len(self.across) > leave:
                dz, copy = self.across.pop(0)
                arrived(copy)
                there = self.block(dz, cols=self.across_cols, part=1 - self.part)
                self.cores.append(remote(there, there, sibling))

    c_out = (c + 8) % 16
    row_q = mult(f * 96, 16)
    own_q = [
        here(
            wqkv_ref.at[:, pl.ds(mult(part * INNER + c * HD, HD), HD)],
            wq.at[pl.ds(row_q, 96), pl.ds(part * HD, HD)])
        for part in range(3)
    ]
    my_cols = pl.ds(mult(core * 768, HD), 768)
    row_o = mult(f * HD, HD)
    own_o = here(wout_ref.at[:, my_cols], wo.at[pl.ds(row_o, HD), my_cols])
    gx = Gather(x_ref, xg)
    qa = Chain(wq, 96, yh, pl.ds(0, 384), pl.ds(384, 384))
    qb = Chain(wq, 96, 1 - yh, pl.ds(0, 384), pl.ds(384, 384))
    ring_cols = pl.ds(mult(core * 768, HD), RING)
    across_cols = pl.ds(mult(core * 768 + RING, HD), 768 - RING)
    oa = WideChain(across_cols, wo, HD, yh, my_cols, my_cols, 0, 64)
    oc = WideChain(across_cols, wo, HD, yh, my_cols, my_cols, 64, 64)
    ob = Chain(wo, HD, 1 - yh, ring_cols, ring_cols)

    for clip in range(CLIPS):
        angle = jnp.full((1, D), time_ref[clip].astype(F32), F32)
        angle = math.pi / 2 * (angle + 0.5) / TIME_STEPS
        sin_t, cos_t = jnp.sin(angle), jnp.cos(angle)
        gains[pl.ds(clip * 3, 1)] = 1.0 + sin_t * tmod_ref[0:1] + cos_t * tmod_ref[1:2]
        gains[pl.ds(clip * 3 + 1, 1)] = 1.0 + sin_t * smod_ref[0:1] + cos_t * smod_ref[1:2]
        gains[pl.ds(clip * 3 + 2, 1)] = cos_t * smod_ref[0:1] - sin_t * smod_ref[1:2]
    within = lax.broadcasted_iota(jnp.int32, (SEG, HD), 0)
    lane0 = lax.broadcasted_iota(jnp.int32, (SEG, HD), 1) == 0
    for clip in range(CLIPS):
        for half in range(2):
            for slot in range(SLOTS):
                token = within + member(slot, half) * SEG
                dead = jnp.logical_and(token >= len_ref[clip], lane0)
                kmask[pl.ds(clip * FULL + half * HALF + slot * SEG, SEG)] = jnp.where(
                    dead, -1e30, 0.0).astype(BF16)
    one0 = jnp.where(lax.broadcasted_iota(jnp.int32, (HALF, HD), 1) == 0, 1.0, 0.0).astype(BF16)

    def project(source, base, out, other):
        y = jnp.dot(source[pl.ds(base, BLK)], wq[...], preferred_element_type=F32).astype(BF16)
        clip, rest = base // HALF, base % HALF
        out[pl.ds(mult(clip * FULL + rest, BLK), BLK)] = y[:, :384]
        other[pl.ds(base, BLK)] = y[:, 384:]

    def modulate(base):
        clip = base // HALF

        def piece(i, _):
            rows = pl.ds(mult(base + i * 32, 32), 32)
            xf = xg[rows].astype(F32)
            rstd = lax.rsqrt(jnp.mean(xf * xf, axis=-1, keepdims=True) + 1e-6)
            normed = xf * rstd
            h_t[rows] = (normed * gains[pl.ds(clip * 3, 1)]).astype(BF16)
            h_s[rows] = (normed * gains[pl.ds(clip * 3 + 1, 1)]).astype(BF16)
            return 0

        lax.fori_loop(0, BLK // 32, piece, 0)

    def exchange(clip, group, out, other):
        return remote(
            other.at[pl.ds(clip * HALF + group * BLK, BLK)],
            out.at[pl.ds(clip * FULL + HALF + group * BLK, BLK)], sibling)

    def send_block(blk, phase, mixed, attn):
        clip, half = blk // 2, blk % 2
        for slot in (7, 4, 5, 6, 3, 1, 2, 0):
            src = mixed.at[pl.ds(blk * HALF + slot * SEG, SEG)]
            dst = attn.at[pl.ds(clip * SEG, SEG), pl.ds(mult(c * HD, HD), HD)]
            if half + slot == 0:
                pltpu.make_async_copy(src, dst, bulk_recv.at[phase]).start()
            else:
                pltpu.make_async_remote_copy(
                    src_ref=src, dst_ref=dst, send_sem=bulk_send.at[phase],
                    recv_sem=bulk_recv.at[phase],
                    device_id=(member(slot, half), f), device_id_type=MESH,
                ).start()

    def send_students():
        cols = pl.ds(mult(c * HD, HD), HD)
        for half in range(2):
            for slot in (7, 4, 5, 6, 3, 1, 2, 0):
                src = mixed_s.at[:, pl.ds(half * HALF + slot * SEG, SEG)]
                dst = attn_s.at[:, :, cols]
                if half + slot == 0:
                    pltpu.make_async_copy(src, dst, bulk_recv.at[1]).start()
                else:
                    pltpu.make_async_remote_copy(
                        src_ref=src, dst_ref=dst, send_sem=bulk_send.at[1],
                        recv_sem=bulk_recv.at[1],
                        device_id=(member(slot, half), f), device_id_type=MESH,
                    ).start()

    def all_received(phase, attn):
        pltpu.make_async_copy(attn, attn, bulk_recv.at[phase]).wait()

    def all_sent(phase, attn):
        part = attn.at[..., pl.ds(0, INNER - HD)]
        pltpu.make_async_copy(part, part, bulk_send.at[phase]).wait()

    NT = (((1,), (1,)), ((), ()))

    def places_of(blk):
        return pl.ds(blk * HALF, HALF), pl.ds(blk // 2 * FULL, FULL)

    def masked_scores(blk, qkv, out):
        rows, keys = places_of(blk)
        query = jnp.concatenate([qkv[rows, 0:HD], one0], axis=1)
        key = jnp.concatenate([qkv[keys, HD:2 * HD], kmask[keys]], axis=1)
        out[...] = lax.dot_general(query, key, NT, preferred_element_type=F32)

    def pipeline(first, second, third, between=lambda stage: None, ready=lambda: None):
        first(0, 0)
        first(1, 1)
        second(0, 0)
        ready()
        first(2, 0)
        second(1, 1)
        third(0, 0)
        between(0)
        first(3, 1)
        second(2, 0)
        third(1, 1)
        between(1)
        second(3, 1)
        third(2, 0)
        third(3, 1)

    score = (score0, score1)
    weigh = (weigh0, weigh1)
    totals = (total0, total1)

    def teacher_scores(blk, p):
        masked_scores(blk, qkv_t, score[p])

    def teacher_softmax(blk, p):
        scores = score[p][...]
        top = jnp.max(scores, axis=-1, keepdims=True)
        expo = jnp.exp2((scores - top) * EXP2_SCALE)
        totals[p][...] = jnp.broadcast_to(jnp.sum(expo, axis=-1, keepdims=True), (HALF, HD))
        weigh[p][...] = expo.astype(BF16)

    def teacher_values(blk, p):
        rows, keys = places_of(blk)
        out = jnp.dot(weigh[p][...], qkv_t[keys, 2 * HD:], preferred_element_type=F32)
        mixed_t[rows] = (out / totals[p][...]).astype(BF16)
        send_block(blk, 0, mixed_t, attn_t)

    def student_block(blk):
        rows, keys = places_of(blk)
        masked_scores(blk, qkv_s, score[0])
        scores = score[0][...]
        top = jnp.max(scores, axis=-1, keepdims=True)
        expo = jnp.exp2((scores - top) * EXP2_SCALE)
        probs = expo * (1.0 / jnp.sum(expo, axis=-1, keepdims=True))
        weights[rows] = probs.astype(BF16)
        scaled[rows] = probs * SCALE
        mixed_s[blk // 2, pl.ds(blk % 2 * HALF, HALF)] = jnp.dot(
            weights[rows], qkv_s[keys, 2 * HD:], preferred_element_type=F32).astype(BF16)

    def tangent_scores(blk, p):
        rows, keys = places_of(blk)
        query = jnp.concatenate([qkv_d[rows, 0:HD], qkv_s[rows, 0:HD]], axis=1)
        key = jnp.concatenate([qkv_s[keys, HD:2 * HD], qkv_d[keys, HD:2 * HD]], axis=1)
        score[p][...] = lax.dot_general(query, key, NT, preferred_element_type=F32)

    def tangent_probs(blk, p):
        rows, keys = places_of(blk)
        dscore = score[p][...]
        prob = scaled[rows]
        mean = jnp.sum(prob * dscore, axis=-1, keepdims=True) * (1.0 / SCALE)
        weigh[p][...] = (prob * (dscore - mean)).astype(BF16)

    def tangent_values(blk, p):
        rows, keys = places_of(blk)
        out = jnp.dot(weigh[p][...], qkv_s[keys, 2 * HD:], preferred_element_type=F32)
        out += jnp.dot(weights[rows], qkv_d[keys, 2 * HD:], preferred_element_type=F32)
        mixed_d[rows] = out.astype(BF16)
        send_block(blk, 2, mixed_d, attn_d)

    def output(attn, out):
        def tile(n, _):
            cols = pl.ds(mult(n * 512, 512), 512)
            out[:, cols] = jnp.dot(
                attn[...].reshape(CLIPS * SEG, INNER), wo[:, cols], preferred_element_type=F32).astype(BF16)
            return 0

        lax.fori_loop(0, 3, tile, 0)

    for copy in own_q:
        copy.wait()
    own_o.wait()
    pl.semaphore_wait(barrier, len(partners))

    qa.step1()
    hop_q = [
        remote(
            wqkv_ref.at[:, pl.ds(mult(part * INNER + c_out * HD, HD), HD)],
            wq.at[pl.ds(row_q, 96), pl.ds(part * HD, HD)], y_out)
        for part in range(3)
    ]
    gx.begin()
    arrived(*hop_q)
    qb.step1()
    qa.step(2)
    gx.step1()
    gx.step2()
    qb.step(2)
    hop_o = remote(
        wo.at[pl.ds(row_o, HD), ring_cols], wo.at[pl.ds(row_o, HD), ring_cols], y_out)
    qa.step(3)
    oa.step1()
    gx.step3()
    qb.step(3)
    oc.step1()
    gx.step4()
    qa.step(4)
    arrived(hop_o)
    ob.step1()
    qb.step(4)
    gx.step5()
    modulate(0)
    qa.last()
    modulate(HALF)
    qb.last()
    oa.step(2)
    oc.step(2)
    qa.end()
    qb.end()

    project(h_t, 0, qkv_t, other_t)
    project(h_t, HALF, qkv_t, other_t)
    swaps_t = [exchange(clip, 0, qkv_t, other_t) for clip in range(2)]
    ob.step(2)
    gx.end_a()
    modulate(BLK)
    project(h_t, BLK, qkv_t, other_t)
    swaps_t.append(exchange(0, 1, qkv_t, other_t))
    gx.end_b()
    modulate(HALF + BLK)
    project(h_t, HALF + BLK, qkv_t, other_t)
    swaps_t.append(exchange(1, 1, qkv_t, other_t))
    oa.step(3)
    oc.step(3)
    project(h_s, 0, qkv_s, other_s)
    swaps_s = [exchange(0, 0, qkv_s, other_s)]
    arrived(*swaps_t)

    def between(stage):
        if stage == 0:
            ob.step(3)
            oa.step(4)
        if stage == 1:
            oc.step(4)

    pipeline(teacher_scores, teacher_softmax, teacher_values, between)
    ob.step(4)
    project(h_s, HALF, qkv_s, other_s)
    swaps_s.append(exchange(1, 0, qkv_s, other_s))
    oa.last()
    project(h_s, BLK, qkv_s, other_s)
    oc.last()
    project(h_s, HALF + BLK, qkv_s, other_s)
    swaps_s += [exchange(clip, 1, qkv_s, other_s) for clip in range(2)]
    ob.last()
    oa.take()
    oc.take()
    all_received(0, attn_t)
    oa.end()
    oc.end()
    ob.end()
    output(attn_t, vel)

    def dh_piece(i, _):
        rows = pl.ds(mult(i * 32, 32), 32)
        clip = i // 2
        xf = x_ref[rows].astype(F32)
        vf = vel[rows].astype(F32)
        rstd = lax.rsqrt(jnp.mean(xf * xf, axis=-1, keepdims=True) + 1e-6)
        cross = jnp.mean(xf * vf, axis=-1, keepdims=True)
        dnormed = rstd * vf - xf * (rstd * rstd * rstd * cross)
        gain = gains[pl.ds(clip * 3 + 1, 1)]
        dgain = gains[pl.ds(clip * 3 + 2, 1)]
        dh[rows] = (dnormed * gain + xf * rstd * dgain).astype(BF16)
        return 0

    lax.fori_loop(0, 4, dh_piece, 0)
    gd = Gather(dh, dg)
    gd.begin()
    arrived(*swaps_s)
    student_block(0)
    gd.step1()
    gd.step2()
    student_block(1)
    student_block(2)
    gd.step3()
    student_block(3)
    gd.step4()
    gd.step5()
    project(dg, 0, qkv_d, other_d)
    project(dg, HALF, qkv_d, other_d)
    swaps_0 = [exchange(0, 0, qkv_d, other_d)]
    swaps_1 = [exchange(1, 0, qkv_d, other_d)]
    gd.end_a()
    project(dg, BLK, qkv_d, other_d)
    swaps_0.append(exchange(0, 1, qkv_d, other_d))

    def second_clip():
        gd.end_b()
        project(dg, HALF + BLK, qkv_d, other_d)
        swaps_1.append(exchange(1, 1, qkv_d, other_d))
        send_students()
        arrived(*swaps_1)

    arrived(*swaps_0)
    pipeline(tangent_scores, tangent_probs, tangent_values, ready=second_clip)
    all_received(1, attn_s)
    output(attn_s, student_ref)
    all_received(2, attn_d)
    output(attn_d, tangent_ref)

    for copy in started:
        copy.wait_send()
    for phase, attn in enumerate((attn_t, attn_s, attn_d)):
        all_sent(phase, attn)


def hand_over(student_ref, tangent_ref, student_out, tangent_out):
    student_out[...] = student_ref[...]
    tangent_out[...] = tangent_ref[...]


def on_device(x_t, clip_len, time_idx, teacher_mod, student_mod, w_qkv, w_out):
    vmem = pl.BlockSpec(memory_space=pltpu.VMEM)
    smem = pl.BlockSpec(memory_space=pltpu.SMEM)
    hbm = pl.BlockSpec(memory_space=pl.ANY)
    rows = CLIPS * SEG
    out = jax.ShapeDtypeStruct((rows, D), BF16)

    def buf(*shape, dtype=BF16):
        return pltpu.VMEM(shape, dtype)

    scratch = [
        buf(CLIPS * HALF, D), buf(CLIPS * HALF, D), buf(D, 768), buf(INNER, D),
        buf(CLIPS * FULL, 384), buf(CLIPS * FULL, 384), buf(CLIPS * FULL, 384),
        buf(CLIPS * HALF, 384), buf(CLIPS * HALF, 384), buf(CLIPS * HALF, 384),
        buf(CLIPS * HALF, D), buf(CLIPS * HALF, D), buf(8, D, dtype=F32), buf(CLIPS * FULL, HD),
        buf(CLIPS * FULL, HD), buf(CLIPS, FULL, HD), buf(CLIPS * FULL, HD),
        buf(rows, INNER), buf(CLIPS, SEG, INNER), buf(rows, INNER),
        buf(rows, D), buf(rows, D),
        buf(CLIPS * FULL, FULL, dtype=F32), buf(CLIPS * FULL, FULL),
        buf(HALF, FULL, dtype=F32), buf(HALF, FULL, dtype=F32), buf(HALF, FULL), buf(HALF, FULL),
        buf(HALF, HD, dtype=F32), buf(HALF, HD, dtype=F32),
        pltpu.SemaphoreType.DMA((192,)), pltpu.SemaphoreType.DMA((192,)),
        pltpu.SemaphoreType.DMA((8,)), pltpu.SemaphoreType.DMA((3,)), pltpu.SemaphoreType.DMA((3,)),
    ]
    student, tangent = pl.pallas_call(
        kernel,
        out_shape=(out, out),
        in_specs=[smem, smem, vmem, vmem, vmem, hbm, hbm],
        out_specs=(vmem, vmem),
        scratch_shapes=scratch,
        compiler_params=pltpu.CompilerParams(
            collective_id=0, has_side_effects=True, vmem_limit_bytes=60 * 2**20),
    )(clip_len, time_idx, x_t.reshape(rows, D), teacher_mod, student_mod, w_qkv, w_out)
    student, tangent = pl.pallas_call(
        hand_over,
        out_shape=(out, out),
        in_specs=[vmem, vmem],
        out_specs=(vmem, vmem),
    )(student, tangent)
    return (student.reshape(CLIPS, SEG, D), tangent.reshape(CLIPS, SEG, D))


def solution(mesh):
    in_specs = (
        P("fsdp", "ctx", None), P("fsdp"), P("fsdp"), P(), P(), P("fsdp", None), P("fsdp", None),
    )
    out_specs = (P("fsdp", "ctx", None), P("fsdp", "ctx", None))
    return jax.shard_map(
        on_device, mesh=mesh, in_specs=in_specs, out_specs=out_specs, check_vma=False)
```

```python
import functools
import math

import jax
import jax.numpy as jnp
from jax import lax
from jax.experimental import pallas as pl
from jax.experimental.pallas import tpu as pltpu
from jax.sharding import PartitionSpec as P

HEADS = 16
HD = 128
TIME_STEPS = 1000
D = 1536
INNER = HEADS * HD
SEG = 64
CLIPS = 2
SLOTS = 8
HALF = SLOTS * SEG
FULL = 2 * HALF
BLK = 4 * SEG
SCALE = 1.0 / math.sqrt(HD)
EXP2_SCALE = SCALE * math.log2(math.e)
MESH = pl.DeviceIdType.MESH
F32 = jnp.float32
BF16 = jnp.bfloat16

RING = 384

S00, S01, S03, S10, S02, S11, S13, S12 = range(8)


PLACES = ((0, 0), (0, 1), (0, 3), (1, 0), (0, 2), (1, 1), (1, 3), (1, 2))


def mult(value, by):
    return pl.multiple_of(value, by)


def kernel(
    len_ref, time_ref, x_ref, tmod_ref, smod_ref, wqkv_ref, wout_ref,
    student_ref, tangent_ref,
    xg, dg, wq, wo, qkv_t, qkv_s, qkv_d, other_t, other_s, other_d, h_t, h_s, gains, kmask,
    mixed_t, mixed_s, mixed_d, attn_t, attn_s, attn_d, vel, dh, scaled, weights,
    score0, score1, weigh0, weigh1, total0, total1,
    send, recv, local, bulk_send, bulk_recv,
):
    c = lax.axis_index("ctx")
    f = lax.axis_index("fsdp")
    core = c % 2
    chip = c // 2
    xx = chip % 4
    yl = c // 8
    z = f // 2
    yh = f % 2

    chips = [((yl + dyl) % 2 * 4 + (xx + dx) % 4) * 2 for dyl, dx in PLACES]
    halves = (core, 1 - core)
    columns = [(z + dz) % 8 * 2 for dz in range(8)]

    def member(slot, half):
        return chips[slot] + halves[half]

    sibling = (member(S00, 1), f)
    x_up, x_down = (member(S01, 0), f), (member(S03, 0), f)
    y_in = (member(S10, 0), f)
    y_out = (member(S10, 0), columns[0] + 1 - yh)
    z_up, z_down = (c, columns[1] + yh), (c, columns[7] + yh)

    barrier = pltpu.get_barrier_semaphore()
    partners = [y_out, z_up, z_down]
    for slot in range(SLOTS):
        for half in range(2):
            if slot + half:
                partners.append((member(slot, half), f))
    for partner in partners:
        pl.semaphore_signal(barrier, inc=1, device_id=partner, device_id_type=MESH)

    used = [0]
    started = []

    def remote(src, dst, where):
        number = used[0]
        used[0] += 1
        copy = pltpu.make_async_remote_copy(
            src_ref=src, dst_ref=dst, send_sem=send.at[number], recv_sem=recv.at[number],
            device_id=where, device_id_type=MESH,
        )
        copy.start()
        started.append(copy)
        return copy

    nlocal = [0]

    def here(src, dst):
        copy = pltpu.make_async_copy(src, dst, local.at[nlocal[0]])
        nlocal[0] += 1
        copy.start()
        return copy

    def arrived(*copies):
        for copy in copies:
            copy.wait_recv()

    class Gather:
        def __init__(self, own, buf):
            self.own, self.buf = own, buf

        def slot(self, clip, slot, lo=0, n=SEG):
            return self.buf.at[pl.ds(clip * HALF + slot * SEG + lo, n)]

        def mine(self, clip):
            return self.own.at[pl.ds(clip * SEG, SEG)]

        def begin(self):
            self.b_up = remote(self.mine(1), self.slot(1, S03), x_up)
            self.b_down = remote(self.mine(1), self.slot(1, S01), x_down)
            self.a_y = remote(self.mine(0), self.slot(0, S10), y_in)
            self.a_up = remote(self.mine(0), self.slot(0, S03), x_up)
            self.a_down = remote(self.mine(0), self.slot(0, S01), x_down)
            self.b_y = remote(self.mine(1), self.slot(1, S10), y_in)
            self.self0 = here(self.mine(0), self.slot(0, S00))
            self.self1 = here(self.mine(1), self.slot(1, S00))

        def step1(self):
            arrived(self.b_up)
            self.b_h_up = remote(self.slot(1, S03, 0, 32), self.slot(1, S02, 0, 32), x_up)
            arrived(self.b_down)
            self.b_h_down = remote(self.slot(1, S01, 32, 32), self.slot(1, S02, 32, 32), x_down)
            self.b_y1 = remote(self.slot(1, S01), self.slot(1, S11), y_in)
            self.b_y3 = remote(self.slot(1, S03), self.slot(1, S13), y_in)

        def step2(self):
            arrived(self.a_y)
            self.a_y_up = remote(self.slot(0, S10), self.slot(0, S13), x_up)
            self.a_y_down = remote(self.slot(0, S10), self.slot(0, S11), x_down)

        def step3(self):
            arrived(self.a_up)
            self.a_h_up = remote(self.slot(0, S03, 0, 32), self.slot(0, S02, 0, 32), x_up)
            arrived(self.a_down)
            self.a_h_down = remote(self.slot(0, S01, 32, 32), self.slot(0, S02, 32, 32), x_down)

        def step4(self):
            arrived(self.b_h_up, self.b_h_down)
            self.b_y2 = remote(self.slot(1, S02), self.slot(1, S12), y_in)
            arrived(self.b_y)
            self.self0.wait()
            self.self1.wait()

        def step5(self):
            arrived(self.a_y_up)
            self.a_yh_up = remote(self.slot(0, S13, 0, 32), self.slot(0, S12, 0, 32), x_up)
            arrived(self.a_y_down)
            self.a_yh_down = remote(self.slot(0, S11, 32, 32), self.slot(0, S12, 32, 32), x_down)

        def end_a(self):
            arrived(self.a_h_up, self.a_h_down, self.a_yh_up, self.a_yh_down)

        def end_b(self):
            arrived(self.b_y1, self.b_y3, self.b_y2)

    class Chain:
        def __init__(self, buf, rows, part, cols, core_cols, first=0, count=None):
            self.buf, self.rows, self.part = buf, rows, part
            self.first, self.count = first, count or rows
            self.cols, self.core_cols = cols, core_cols
            self.cores = []

        def block(self, dz, lo=0, n=None, cols=None, part=None):
            at = columns[dz % 8] + (self.part if part is None else part)
            base = mult(at * self.rows + self.first + lo, 16)
            return self.buf.at[pl.ds(base, n or self.count), self.cols if cols is None else cols]

        def share(self, dz):
            self.cores.append(remote(
                self.block(dz), self.block(dz, cols=self.core_cols), sibling))

        def step1(self):
            self.up = remote(self.block(0), self.block(0), z_up)
            self.down = remote(self.block(0), self.block(0), z_down)
            self.share(0)

        def step(self, k):
            half = self.count // 2
            arrived(self.up)
            lo, n = (0, half) if k == 4 else (0, self.count)
            self.up = remote(self.block(9 - k, lo, n), self.block(9 - k, lo, n), z_up)
            arrived(self.down)
            lo, n = (half, half) if k == 4 else (0, self.count)
            self.down = remote(self.block(k - 1, lo, n), self.block(k - 1, lo, n), z_down)
            self.share(9 - k)
            self.share(k - 1)

        def last(self):
            arrived(self.up, self.down)
            self.share(4)

        def end(self):
            arrived(*self.cores)

    class WideChain(Chain):
        def __init__(self, across_cols, *args):
            super().__init__(*args)
            self.across_cols, self.across = across_cols, []

        def share(self, dz):
            across = self.block(dz, cols=self.across_cols)
            self.across.append((dz, remote(across, across, y_out)))
            super().share(dz)

        def take(self, leave=0):
            while len(self.across) > leave:
                dz, copy = self.across.pop(0)
                arrived(copy)
                there = self.block(dz, cols=self.across_cols, part=1 - self.part)
                self.cores.append(remote(there, there, sibling))

    c_out = (c + 8) % 16
    row_q = mult(f * 96, 16)
    own_q = [
        here(
            wqkv_ref.at[:, pl.ds(mult(part * INNER + c * HD, HD), HD)],
            wq.at[pl.ds(row_q, 96), pl.ds(part * HD, HD)])
        for part in range(3)
    ]
    my_cols = pl.ds(mult(core * 768, HD), 768)
    row_o = mult(f * HD, HD)
    own_o = here(wout_ref.at[:, my_cols], wo.at[pl.ds(row_o, HD), my_cols])
    gx = Gather(x_ref, xg)
    qa = Chain(wq, 96, yh, pl.ds(0, 384), pl.ds(384, 384))
    qb = Chain(wq, 96, 1 - yh, pl.ds(0, 384), pl.ds(384, 384))
    ring_cols = pl.ds(mult(core * 768, HD), RING)
    across_cols = pl.ds(mult(core * 768 + RING, HD), 768 - RING)
    oa = WideChain(across_cols, wo, HD, yh, my_cols, my_cols, 0, 64)
    oc = WideChain(across_cols, wo, HD, yh, my_cols, my_cols, 64, 64)
    ob = Chain(wo, HD, 1 - yh, ring_cols, ring_cols)

    for clip in range(CLIPS):
        angle = jnp.full((1, D), time_ref[clip].astype(F32), F32)
        angle = math.pi / 2 * (angle + 0.5) / TIME_STEPS
        sin_t, cos_t = jnp.sin(angle), jnp.cos(angle)
        gains[pl.ds(clip * 3, 1)] = 1.0 + sin_t * tmod_ref[0:1] + cos_t * tmod_ref[1:2]
        gains[pl.ds(clip * 3 + 1, 1)] = 1.0 + sin_t * smod_ref[0:1] + cos_t * smod_ref[1:2]
        gains[pl.ds(clip * 3 + 2, 1)] = cos_t * smod_ref[0:1] - sin_t * smod_ref[1:2]
    within = lax.broadcasted_iota(jnp.int32, (SEG, HD), 0)
    lane0 = lax.broadcasted_iota(jnp.int32, (SEG, HD), 1) == 0
    for clip in range(CLIPS):
        for half in range(2):
            for slot in range(SLOTS):
                token = within + member(slot, half) * SEG
                dead = jnp.logical_and(token >= len_ref[clip], lane0)
                kmask[pl.ds(clip * FULL + half * HALF + slot * SEG, SEG)] = jnp.where(
                    dead, -1e30, 0.0).astype(BF16)
    one0 = jnp.where(lax.broadcasted_iota(jnp.int32, (HALF, HD), 1) == 0, 1.0, 0.0).astype(BF16)

    def project(source, base, out, other):
        y = jnp.dot(source[pl.ds(base, BLK)], wq[...], preferred_element_type=F32).astype(BF16)
        clip, rest = base // HALF, base % HALF
        out[pl.ds(mult(clip * FULL + rest, BLK), BLK)] = y[:, :384]
        other[pl.ds(base, BLK)] = y[:, 384:]

    def modulate(base):
        clip = base // HALF

        def piece(i, _):
            rows = pl.ds(mult(base + i * 32, 32), 32)
            xf = xg[rows].astype(F32)
            rstd = lax.rsqrt(jnp.mean(xf * xf, axis=-1, keepdims=True) + 1e-6)
            normed = xf * rstd
            h_t[rows] = (normed * gains[pl.ds(clip * 3, 1)]).astype(BF16)
            h_s[rows] = (normed * gains[pl.ds(clip * 3 + 1, 1)]).astype(BF16)
            return 0

        lax.fori_loop(0, BLK // 32, piece, 0)

    def exchange(clip, group, out, other):
        return remote(
            other.at[pl.ds(clip * HALF + group * BLK, BLK)],
            out.at[pl.ds(clip * FULL + HALF + group * BLK, BLK)], sibling)

    def send_block(blk, phase, mixed, attn):
        clip, half = blk // 2, blk % 2
        for slot in (7, 4, 5, 6, 3, 1, 2, 0):
            src = mixed.at[pl.ds(blk * HALF + slot * SEG, SEG)]
            dst = attn.at[pl.ds(clip * SEG, SEG), pl.ds(mult(c * HD, HD), HD)]
            if half + slot == 0:
                pltpu.make_async_copy(src, dst, bulk_recv.at[phase]).start()
            else:
                pltpu.make_async_remote_copy(
                    src_ref=src, dst_ref=dst, send_sem=bulk_send.at[phase],
                    recv_sem=bulk_recv.at[phase],
                    device_id=(member(slot, half), f), device_id_type=MESH,
                ).start()

    def send_students():
        cols = pl.ds(mult(c * HD, HD), HD)
        for half in range(2):
            for slot in (7, 4, 5, 6, 3, 1, 2, 0):
                src = mixed_s.at[:, pl.ds(half * HALF + slot * SEG, SEG)]
                dst = attn_s.at[:, :, cols]
                if half + slot == 0:
                    pltpu.make_async_copy(src, dst, bulk_recv.at[1]).start()
                else:
                    pltpu.make_async_remote_copy(
                        src_ref=src, dst_ref=dst, send_sem=bulk_send.at[1],
                        recv_sem=bulk_recv.at[1],
                        device_id=(member(slot, half), f), device_id_type=MESH,
                    ).start()

    def all_received(phase, attn):
        pltpu.make_async_copy(attn, attn, bulk_recv.at[phase]).wait()

    def all_sent(phase, attn):
        part = attn.at[..., pl.ds(0, INNER - HD)]
        pltpu.make_async_copy(part, part, bulk_send.at[phase]).wait()

    NT = (((1,), (1,)), ((), ()))

    def places_of(blk):
        return pl.ds(blk * HALF, HALF), pl.ds(blk // 2 * FULL, FULL)

    def masked_scores(blk, qkv, out):
        rows, keys = places_of(blk)
        query = jnp.concatenate([qkv[rows, 0:HD], one0], axis=1)
        key = jnp.concatenate([qkv[keys, HD:2 * HD], kmask[keys]], axis=1)
        out[...] = lax.dot_general(query, key, NT, preferred_element_type=F32)

    def pipeline(first, second, third, between=lambda stage: None):
        first(0, 0)
        first(1, 1)
        second(0, 0)
        first(2, 0)
        second(1, 1)
        third(0, 0)
        between(0)
        first(3, 1)
        second(2, 0)
        third(1, 1)
        between(1)
        second(3, 1)
        third(2, 0)
        third(3, 1)

    score = (score0, score1)
    weigh = (weigh0, weigh1)
    totals = (total0, total1)

    def teacher_scores(blk, p):
        masked_scores(blk, qkv_t, score[p])

    def teacher_softmax(blk, p):
        scores = score[p][...]
        top = jnp.max(scores, axis=-1, keepdims=True)
        expo = jnp.exp2((scores - top) * EXP2_SCALE)
        totals[p][...] = jnp.broadcast_to(jnp.sum(expo, axis=-1, keepdims=True), (HALF, HD))
        weigh[p][...] = expo.astype(BF16)

    def teacher_values(blk, p):
        rows, keys = places_of(blk)
        out = jnp.dot(weigh[p][...], qkv_t[keys, 2 * HD:], preferred_element_type=F32)
        mixed_t[rows] = (out / totals[p][...]).astype(BF16)
        send_block(blk, 0, mixed_t, attn_t)

    def student_block(blk):
        rows, keys = places_of(blk)
        masked_scores(blk, qkv_s, score[0])
        scores = score[0][...]
        top = jnp.max(scores, axis=-1, keepdims=True)
        expo = jnp.exp2((scores - top) * EXP2_SCALE)
        probs = expo * (1.0 / jnp.sum(expo, axis=-1, keepdims=True))
        weights[rows] = probs.astype(BF16)
        scaled[rows] = probs * SCALE
        mixed_s[blk // 2, pl.ds(blk % 2 * HALF, HALF)] = jnp.dot(
            weights[rows], qkv_s[keys, 2 * HD:], preferred_element_type=F32).astype(BF16)

    def tangent_scores(blk, p):
        rows, keys = places_of(blk)
        query = jnp.concatenate([qkv_d[rows, 0:HD], qkv_s[rows, 0:HD]], axis=1)
        key = jnp.concatenate([qkv_s[keys, HD:2 * HD], qkv_d[keys, HD:2 * HD]], axis=1)
        score[p][...] = lax.dot_general(query, key, NT, preferred_element_type=F32)

    def tangent_probs(blk, p):
        rows, keys = places_of(blk)
        dscore = score[p][...]
        prob = scaled[rows]
        mean = jnp.sum(prob * dscore, axis=-1, keepdims=True) * (1.0 / SCALE)
        weigh[p][...] = (prob * (dscore - mean)).astype(BF16)

    def tangent_values(blk, p):
        rows, keys = places_of(blk)
        out = jnp.dot(weigh[p][...], qkv_s[keys, 2 * HD:], preferred_element_type=F32)
        out += jnp.dot(weights[rows], qkv_d[keys, 2 * HD:], preferred_element_type=F32)
        mixed_d[rows] = out.astype(BF16)
        send_block(blk, 2, mixed_d, attn_d)

    def output(attn, out):
        def tile(n, _):
            cols = pl.ds(mult(n * 512, 512), 512)
            out[:, cols] = jnp.dot(
                attn[...].reshape(CLIPS * SEG, INNER), wo[:, cols], preferred_element_type=F32).astype(BF16)
            return 0

        lax.fori_loop(0, 3, tile, 0)

    for copy in own_q:
        copy.wait()
    own_o.wait()
    pl.semaphore_wait(barrier, len(partners))

    qa.step1()
    hop_q = [
        remote(
            wqkv_ref.at[:, pl.ds(mult(part * INNER + c_out * HD, HD), HD)],
            wq.at[pl.ds(row_q, 96), pl.ds(part * HD, HD)], y_out)
        for part in range(3)
    ]
    gx.begin()
    arrived(*hop_q)
    qb.step1()
    qa.step(2)
    gx.step1()
    gx.step2()
    qb.step(2)
    hop_o = remote(
        wo.at[pl.ds(row_o, HD), ring_cols], wo.at[pl.ds(row_o, HD), ring_cols], y_out)
    qa.step(3)
    oa.step1()
    gx.step3()
    qb.step(3)
    oc.step1()
    gx.step4()
    qa.step(4)
    arrived(hop_o)
    ob.step1()
    qb.step(4)
    gx.step5()
    modulate(0)
    qa.last()
    modulate(HALF)
    qb.last()
    oa.step(2)
    oc.step(2)
    qa.end()
    qb.end()

    project(h_t, 0, qkv_t, other_t)
    project(h_t, HALF, qkv_t, other_t)
    swaps_t = [exchange(clip, 0, qkv_t, other_t) for clip in range(2)]
    ob.step(2)
    gx.end_a()
    modulate(BLK)
    project(h_t, BLK, qkv_t, other_t)
    swaps_t.append(exchange(0, 1, qkv_t, other_t))
    gx.end_b()
    modulate(HALF + BLK)
    project(h_t, HALF + BLK, qkv_t, other_t)
    swaps_t.append(exchange(1, 1, qkv_t, other_t))
    oa.step(3)
    oc.step(3)
    project(h_s, 0, qkv_s, other_s)
    swaps_s = [exchange(0, 0, qkv_s, other_s)]
    arrived(*swaps_t)

    def between(stage):
        if stage == 0:
            ob.step(3)
            oa.step(4)
        if stage == 1:
            oc.step(4)

    pipeline(teacher_scores, teacher_softmax, teacher_values, between)
    ob.step(4)
    project(h_s, HALF, qkv_s, other_s)
    swaps_s.append(exchange(1, 0, qkv_s, other_s))
    oa.last()
    project(h_s, BLK, qkv_s, other_s)
    oc.last()
    project(h_s, HALF + BLK, qkv_s, other_s)
    swaps_s += [exchange(clip, 1, qkv_s, other_s) for clip in range(2)]
    ob.last()
    oa.take()
    oc.take()
    all_received(0, attn_t)
    oa.end()
    oc.end()
    ob.end()
    output(attn_t, vel)

    def dh_piece(i, _):
        rows = pl.ds(mult(i * 32, 32), 32)
        clip = i // 2
        xf = x_ref[rows].astype(F32)
        vf = vel[rows].astype(F32)
        rstd = lax.rsqrt(jnp.mean(xf * xf, axis=-1, keepdims=True) + 1e-6)
        cross = jnp.mean(xf * vf, axis=-1, keepdims=True)
        dnormed = rstd * vf - xf * (rstd * rstd * rstd * cross)
        gain = gains[pl.ds(clip * 3 + 1, 1)]
        dgain = gains[pl.ds(clip * 3 + 2, 1)]
        dh[rows] = (dnormed * gain + xf * rstd * dgain).astype(BF16)
        return 0

    lax.fori_loop(0, 4, dh_piece, 0)
    gd = Gather(dh, dg)
    gd.begin()
    arrived(*swaps_s)
    student_block(0)
    gd.step1()
    gd.step2()
    student_block(1)
    student_block(2)
    gd.step3()
    student_block(3)
    gd.step4()
    gd.step5()
    project(dg, 0, qkv_d, other_d)
    project(dg, HALF, qkv_d, other_d)
    swaps_d = [exchange(clip, 0, qkv_d, other_d) for clip in range(2)]
    gd.end_a()
    project(dg, BLK, qkv_d, other_d)
    swaps_d.append(exchange(0, 1, qkv_d, other_d))
    gd.end_b()
    project(dg, HALF + BLK, qkv_d, other_d)
    swaps_d.append(exchange(1, 1, qkv_d, other_d))
    send_students()
    arrived(*swaps_d)
    pipeline(tangent_scores, tangent_probs, tangent_values)
    all_received(1, attn_s)
    output(attn_s, student_ref)
    all_received(2, attn_d)
    output(attn_d, tangent_ref)

    for copy in started:
        copy.wait_send()
    for phase, attn in enumerate((attn_t, attn_s, attn_d)):
        all_sent(phase, attn)


def hand_over(student_ref, tangent_ref, student_out, tangent_out):
    student_out[...] = student_ref[...]
    tangent_out[...] = tangent_ref[...]


def on_device(x_t, clip_len, time_idx, teacher_mod, student_mod, w_qkv, w_out):
    vmem = pl.BlockSpec(memory_space=pltpu.VMEM)
    smem = pl.BlockSpec(memory_space=pltpu.SMEM)
    hbm = pl.BlockSpec(memory_space=pl.ANY)
    rows = CLIPS * SEG
    out = jax.ShapeDtypeStruct((rows, D), BF16)

    def buf(*shape, dtype=BF16):
        return pltpu.VMEM(shape, dtype)

    scratch = [
        buf(CLIPS * HALF, D), buf(CLIPS * HALF, D), buf(D, 768), buf(INNER, D),
        buf(CLIPS * FULL, 384), buf(CLIPS * FULL, 384), buf(CLIPS * FULL, 384),
        buf(CLIPS * HALF, 384), buf(CLIPS * HALF, 384), buf(CLIPS * HALF, 384),
        buf(CLIPS * HALF, D), buf(CLIPS * HALF, D), buf(8, D, dtype=F32), buf(CLIPS * FULL, HD),
        buf(CLIPS * FULL, HD), buf(CLIPS, FULL, HD), buf(CLIPS * FULL, HD),
        buf(rows, INNER), buf(CLIPS, SEG, INNER), buf(rows, INNER),
        buf(rows, D), buf(rows, D),
        buf(CLIPS * FULL, FULL, dtype=F32), buf(CLIPS * FULL, FULL),
        buf(HALF, FULL, dtype=F32), buf(HALF, FULL, dtype=F32), buf(HALF, FULL), buf(HALF, FULL),
        buf(HALF, HD, dtype=F32), buf(HALF, HD, dtype=F32),
        pltpu.SemaphoreType.DMA((192,)), pltpu.SemaphoreType.DMA((192,)),
        pltpu.SemaphoreType.DMA((8,)), pltpu.SemaphoreType.DMA((3,)), pltpu.SemaphoreType.DMA((3,)),
    ]
    student, tangent = pl.pallas_call(
        kernel,
        out_shape=(out, out),
        in_specs=[smem, smem, vmem, vmem, vmem, hbm, hbm],
        out_specs=(vmem, vmem),
        scratch_shapes=scratch,
        compiler_params=pltpu.CompilerParams(
            collective_id=0, has_side_effects=True, vmem_limit_bytes=60 * 2**20),
    )(clip_len, time_idx, x_t.reshape(rows, D), teacher_mod, student_mod, w_qkv, w_out)
    student, tangent = pl.pallas_call(
        hand_over,
        out_shape=(out, out),
        in_specs=[vmem, vmem],
        out_specs=(vmem, vmem),
    )(student, tangent)
    return (student.reshape(CLIPS, SEG, D), tangent.reshape(CLIPS, SEG, D))


def solution(mesh):
    in_specs = (
        P("fsdp", "ctx", None), P("fsdp"), P("fsdp"), P(), P(), P("fsdp", None), P("fsdp", None),
    )
    out_specs = (P("fsdp", "ctx", None), P("fsdp", "ctx", None))
    return jax.shard_map(
        on_device, mesh=mesh, in_specs=in_specs, out_specs=out_specs, check_vma=False)
```
